32 devices in a mesh: seq: 8 (over z, x), head: 4 (over y, core).
Axes of the slice: x: 2, y: 2, z: 4, core: 2. Of those that a mesh axis runs over, the one named last changes fastest.
Arguments:
- queries: bfloat16 [4096, 4096], P('seq', 'head'), may hold values from -6 to 6
- keys: bfloat16 [4096, 4096], P('seq', 'head'), may hold values from -6 to 6
- values: bfloat16 [4096, 4096], P('seq', 'head'), may hold values from -6 to 6
- log_decay: float32 [32, 4096], P('head', 'seq'), may hold values from -3 to 0
- beta: float32 [32, 4096], P('head', 'seq'), may hold values from 0.001 to 0.03
- level_weights: float32 [10, 32, 4096], P(None, 'head', 'seq'), may hold values from 0.25 to 2
- doc_start: int32 [64], P('seq'), may hold values from 0 to 1, as said below
- norm_gain: float32 [4096], P('head'), may hold values from 0.25 to 1.75
- out_weight: bfloat16 [4096, 4096], P('head'), may hold values from -0.09375 to 0.09375
Outputs:
- mixed: bfloat16 [4096, 4096], P(('seq', 'head'))
The draws below stay inside these ranges and needn't reach their ends.
Inputs may be any that keep to these rules, and one draw needn't show every extreme that they name: doc_start is 0 on the first 32 spans; the second half holds at least one 1.
All inputs are finite; a program needn't handle non-finite values.
Results may differ from the reference program's by a relative error of at most 0.014.
Values may be sent and summed in bfloat16 or wider, within the bound.
A program may use at most 128 MiB of HBM per device.

```python
import math
import jax
import jax.numpy as jnp
import numpy as np
from jax import lax

D = 4096
HEADS = 32
HEAD_DIM = 128
SPAN = 64
LEVELS = 10
TOK_DEV = 512
TOKENS = 4096
WIDTH = 4096
NCHUNKS = 64
N_SEQ = 8
N_HEAD = 4


def shared_direction(key):
    return jax.random.truncated_normal(jax.random.fold_in(key, 101), -4.0, 4.0, (WIDTH,), jnp.float32)


def draw_queries(key, part):
    amount = 0.6
    noise = jax.random.truncated_normal(jax.random.fold_in(key, 211), -5.0, 5.0, (TOKENS, WIDTH), jnp.float32)
    return jnp.clip(amount * shared_direction(key)[None, :] + noise, -6.0, 6.0).astype(jnp.bfloat16)


def draw_keys(key, part):
    amount = 0.6
    noise = jax.random.truncated_normal(jax.random.fold_in(key, 307), -5.0, 5.0, (TOKENS, WIDTH), jnp.float32)
    return jnp.clip(amount * shared_direction(key)[None, :] + noise, -6.0, 6.0).astype(jnp.bfloat16)


def draw_log_decay(key, part):
    keys_list = jax.random.split(key, 7)
    slow_share = 0.5
    slow = jax.random.uniform(keys_list[0], (HEADS, 1)) < slow_share
    slow_rate = jnp.exp(jax.random.uniform(keys_list[1], (HEADS, 1), jnp.float32, math.log(0.05), math.log(0.6))) / TOKENS
    fast_rate = jnp.exp(jax.random.uniform(keys_list[2], (HEADS, 1), jnp.float32, math.log(1.0 / 50.0), math.log(1.0 / 30.0)))
    forgetting_rate = jnp.where(slow, slow_rate, fast_rate)
    segment_scaling_factor = jnp.exp(jax.random.uniform(keys_list[3], (HEADS, TOKENS // TOK_DEV), jnp.float32, math.log(0.5), math.log(2.0)))
    segment_scaling_factor = jnp.repeat(segment_scaling_factor, TOK_DEV, axis=1)
    stochastic_shift = jax.random.uniform(keys_list[4], (HEADS, TOKENS), jnp.float32, 0.5, 1.5)
    spots = jax.random.randint(keys_list[5], (4,), 0, TOKENS)
    omitted_elements = jax.random.uniform(keys_list[6], (4, 1), jnp.float32, math.log(0.5), math.log(0.8))
    index_sequence = jnp.arange(TOKENS)[None, :] == spots[:, None]
    clustered_occurrences = jnp.sum(jnp.where(index_sequence, omitted_elements, 0.0), axis=0)
    return (-forgetting_rate * segment_scaling_factor * stochastic_shift + clustered_occurrences[None, :]).astype(jnp.float32)


def draw_doc_start(key, part):
    keys_list = jax.random.split(jax.random.fold_in(key, 17), 2)
    half_count = NCHUNKS // 2
    positions = jnp.arange(NCHUNKS, dtype=jnp.int32)
    random_starts = jax.random.randint(keys_list[0], (NCHUNKS,), 0, 8) == 0
    forced_spot = half_count + jax.random.randint(keys_list[1], (), 0, NCHUNKS - half_count)
    flagged = random_starts & (positions >= half_count) | (positions == forced_spot)
    return flagged.astype(jnp.int32)


def shard_levels(stream_key, extent, cuts, least, high):
    loudness = 1.0
    for position, blocks in cuts:
        heights = jax.random.uniform(jax.random.fold_in(jax.random.fold_in(stream_key, 6), position), (blocks,), jnp.float32, least / len(cuts), high / len(cuts))
        loudness = loudness * jnp.repeat(jnp.exp(heights), extent[position] // blocks).reshape((-1,) + (1,) * (len(extent) - 1 - position))
    return loudness


def centred(key, dims, scale, bound, shards=(), kind=jnp.bfloat16):
    drawn = jax.random.normal(key, dims, jnp.float32) * scale
    if len(shards) > 0:
        drawn = shard_levels(key, dims, shards, -0.22, 0.18) * drawn
    return jnp.clip(drawn, min=-bound, max=bound).astype(kind)


def setup_inputs(seed: int = 0) -> dict:
    key_of = jax.random.split(jax.random.key(seed), 10)
    return {
        "queries": draw_queries(jax.random.fold_in(key_of[9], 71), 0),
        "keys": draw_keys(jax.random.fold_in(key_of[9], 71), 0),
        "values": centred(key_of[2], (TOKENS, WIDTH), 1.0, 6.0, ((0, 8), (1, 4))),
        "log_decay": draw_log_decay(jax.random.fold_in(key_of[9], 71), 0),
        "beta": jnp.clip(jnp.exp(math.log(0.03) - 3.4011973 * jax.random.uniform(key_of[4], (HEADS, TOKENS), jnp.float32) ** shard_levels(key_of[4], (HEADS, TOKENS), ((0, 4), (1, 8)), -0.2, 0.2)), 0.001, 0.03),
        "level_weights": jnp.clip(jnp.exp(math.log(2.0) - 2.0794415 * jax.random.uniform(key_of[5], (LEVELS, HEADS, TOKENS), jnp.float32) ** shard_levels(key_of[5], (LEVELS, HEADS, TOKENS), ((1, 4), (2, 8)), -0.2, 0.2)), 0.25, 2.0),
        "doc_start": draw_doc_start(jax.random.fold_in(key_of[9], 71), 0),
        "norm_gain": jnp.clip(1.0 + 0.15 * jax.random.normal(key_of[7], (WIDTH,), jnp.float32), 0.25, 1.75),
        "out_weight": centred(key_of[8], (WIDTH, D), WIDTH ** -0.5, 0.09375, ((0, 4),)),
    }


HIGH = lax.Precision.HIGHEST

def normalize(vector):
    return vector / jnp.sqrt(lax.optimization_barrier(jnp.sum(vector * vector, axis=-1, keepdims=True)) + 1e-06)

def compose(first, second):
    first_t, first_s = first
    second_token, second_s = second
    new_t = jnp.einsum('...de,...ef->...df', second_token, first_t, precision=HIGH)
    new_s = jnp.einsum('...de,...ef->...df', second_token, first_s, precision=HIGH) + second_s
    return (new_t, new_s)

def unit_lower_inverse(lower_part):
    span_len = lower_part.shape[-1]
    identity_span = jnp.eye(span_len, dtype=jnp.float32)
    power = -lower_part
    inverse = identity_span + power
    reach = 2
    while reach < span_len:
        power = jnp.einsum('...ij,...jk->...ik', power, power, precision=HIGH)
        inverse = jnp.einsum('...ij,...jk->...ik', inverse, identity_span + power, precision=HIGH)
        reach = reach * 2
    return inverse

def span_terms(query_c, key_c, value_c, log_c, beta_c):
    span_len = query_c.shape[-2]
    head_dim = query_c.shape[-1]
    cum_log = jnp.cumsum(log_c, axis=-1)
    gamma = jnp.exp(cum_log)
    row_ids = lax.broadcasted_iota(jnp.int32, (span_len, span_len), 0)
    col_ids = lax.broadcasted_iota(jnp.int32, (span_len, span_len), 1)
    inclusive = row_ids >= col_ids
    exacting_mode = row_ids > col_ids
    spread = cum_log[..., :, None] - cum_log[..., None, :]
    ratio = jnp.where(inclusive, jnp.exp(jnp.where(inclusive, spread, 0.0)), 0.0)
    key_key = jnp.einsum('...id,...jd->...ij', key_c, key_c, precision=HIGH)
    lower_part = jnp.where(exacting_mode, beta_c[..., :, None] * ratio * key_key, 0.0)
    rhs = jnp.concatenate([beta_c[..., None] * value_c, (beta_c * gamma)[..., None] * key_c], axis=-1)
    solved = jnp.einsum('...ij,...jd->...id', unit_lower_inverse(lower_part), rhs, precision=HIGH)
    new_values = solved[..., :head_dim]
    erasers = solved[..., head_dim:]
    scores = ratio * jnp.einsum('...id,...jd->...ij', query_c, key_c, precision=HIGH)
    reader = gamma[..., None] * query_c - jnp.einsum('...ij,...jd->...id', scores, erasers, precision=HIGH)
    intra = jnp.einsum('...ij,...jd->...id', scores, new_values, precision=HIGH)
    tail_keys = jnp.exp(cum_log[..., -1:] - cum_log)[..., None] * key_c
    identity_mat = jnp.eye(head_dim, dtype=jnp.float32)
    trans = gamma[..., -1][..., None, None] * identity_mat - jnp.einsum('...jd,...je->...de', tail_keys, erasers, precision=HIGH)
    write = jnp.einsum('...jd,...je->...de', tail_keys, new_values, precision=HIGH)
    return (reader, intra, trans, write)

def prepare(query_b, key_b, value_b, log_b, beta_b, weight_b, flags):
    tokens = query_b.shape[0]
    heads = log_b.shape[0]
    head_dim = query_b.shape[1] // heads
    count = tokens // SPAN

    def split_rows(matrix):
        return matrix.astype(jnp.float32).reshape(count, SPAN, heads, head_dim).transpose(0, 2, 1, 3)
    query_c = normalize(split_rows(query_b))
    key_c = normalize(split_rows(key_b))
    value_c = split_rows(value_b)
    log_c = log_b.reshape(heads, count, SPAN).transpose(1, 0, 2)
    beta_c = beta_b.reshape(heads, count, SPAN).transpose(1, 0, 2)
    weight_c = weight_b.reshape(weight_b.shape[0], heads, count, SPAN).transpose(2, 0, 1, 3)
    reader, intra, trans, write = span_terms(query_c, key_c, value_c, log_c, beta_c)
    keep = (1 - flags).astype(jnp.float32)
    return (reader, intra, trans, write, keep, weight_c)

def scan_summary(trans, write, keep):
    heads = trans.shape[1]
    head_dim = trans.shape[2]
    start = (jnp.broadcast_to(jnp.eye(head_dim, dtype=jnp.float32), (heads, head_dim, head_dim)), jnp.zeros((heads, head_dim, head_dim), jnp.float32))

    def step(carry, item):
        trans_c, write_c, keep_c = item
        return (compose(carry, (keep_c * trans_c, write_c)), None)
    return lax.scan(step, start, (trans, write, keep))[0]

def level_states(block_idx, buckets, heads, head_dim, low_levels):
    carried = jnp.broadcast_to(jnp.eye(head_dim, dtype=jnp.float32), (heads, head_dim, head_dim))
    states = [jnp.zeros((heads, head_dim, head_dim), jnp.float32) for level in range(low_levels + 1)]
    for level_bit in range(len(buckets)):
        flagged_binary_digit = block_idx >> level_bit & 1 == 1
        bucket_t, bucket_s = buckets[level_bit]
        states.append(jnp.where(flagged_binary_digit, jnp.einsum('hde,hef->hdf', carried, bucket_s, precision=HIGH), 0.0))
        carried = jnp.where(flagged_binary_digit, jnp.einsum('hde,hef->hdf', carried, bucket_t, precision=HIGH), carried)
    return jnp.stack(states)

def read_levels(reader, intra, trans, write, keep, weight_c, states):
    used = states.shape[0]
    count = reader.shape[0]
    merge_top = np.array([(i + 1 & -(i + 1)).bit_length() - 1 for i in range(count)], dtype=np.int32)
    slots = jnp.arange(used, dtype=jnp.int32)

    def step(carry, item):
        reader_c, intra_c, trans_c, write_c, keep_c, weight_now, top = item
        entering = keep_c * carry
        reads = jnp.einsum('hcd,lhde->lhce', reader_c, entering, precision=HIGH)
        weights = weight_now[:used]
        output = lax.optimization_barrier(jnp.sum(weights[..., None] * reads, axis=0)) + weights[0][..., None] * intra_c
        leaving = jnp.einsum('hde,lhef->lhdf', trans_c, entering, precision=HIGH)
        leaving = leaving.at[0].add(write_c)
        low = (slots <= top)[:, None, None, None]
        combined_levels = lax.optimization_barrier(jnp.sum(jnp.where(low, leaving, 0.0), axis=0))
        target = (slots == top + 1)[:, None, None, None]
        leaving = jnp.where(low, 0.0, leaving) + jnp.where(target, combined_levels[None], 0.0)
        return (leaving, output)
    return lax.scan(step, states, (reader, intra, trans, write, keep, weight_c, jnp.asarray(merge_top)))[1]

def finish(outputs, norm_gain):
    count, heads, span_len, head_dim = outputs.shape
    rows = outputs.transpose(0, 2, 1, 3).reshape(count * span_len, heads, head_dim)
    scaled = rows / jnp.sqrt(lax.optimization_barrier(jnp.mean(rows * rows, axis=-1, keepdims=True)) + 1e-06)
    scaled = scaled * norm_gain.reshape(heads, head_dim)
    return scaled.reshape(count * span_len, heads * head_dim).astype(jnp.bfloat16)

def reference(queries, keys, values, log_decay, beta, level_weights, doc_start, norm_gain, out_weight):
    nbits = N_SEQ.bit_length() - 1
    per_block = TOK_DEV // SPAN
    low_levels = per_block.bit_length() - 1

    def block_terms(block_idx):
        start = block_idx * TOK_DEV
        query_b = lax.dynamic_slice_in_dim(queries, start, TOK_DEV, 0)
        key_b = lax.dynamic_slice_in_dim(keys, start, TOK_DEV, 0)
        value_b = lax.dynamic_slice_in_dim(values, start, TOK_DEV, 0)
        log_b = lax.dynamic_slice_in_dim(log_decay, start, TOK_DEV, 1)
        beta_b = lax.dynamic_slice_in_dim(beta, start, TOK_DEV, 1)
        weight_b = lax.dynamic_slice_in_dim(level_weights, start, TOK_DEV, 2)
        flags = lax.dynamic_slice_in_dim(doc_start, block_idx * per_block, per_block, 0)
        return prepare(query_b, key_b, value_b, log_b, beta_b, weight_b, flags)

    def block_summary(block_idx):
        reader, intra, trans, write, keep, weight_c = block_terms(block_idx)
        return scan_summary(trans, write, keep)
    block_ids = jnp.arange(N_SEQ, dtype=jnp.int32)
    summaries = lax.map(block_summary, block_ids)
    tree = [summaries]
    for level_bit in range(nbits - 1):
        level_t, level_s = tree[-1]
        tree.append(compose((level_t[0::2], level_s[0::2]), (level_t[1::2], level_s[1::2])))
    group_width = WIDTH // N_HEAD

    def block_out(block_idx):
        reader, intra, trans, write, keep, weight_c = block_terms(block_idx)
        buckets = []
        for level_bit in range(nbits):
            sibling = jnp.bitwise_xor(block_idx >> level_bit, 1)
            buckets.append((tree[level_bit][0][sibling], tree[level_bit][1][sibling]))
        states = level_states(block_idx, buckets, HEADS, HEAD_DIM, low_levels)
        outputs = read_levels(reader, intra, trans, write, keep, weight_c, states)
        normed = finish(outputs, norm_gain)
        total = jnp.zeros((TOK_DEV, D), jnp.float32)
        for group in range(N_HEAD):
            partial_value = jnp.dot(normed[:, group * group_width:(group + 1) * group_width], out_weight[group * group_width:(group + 1) * group_width], preferred_element_type=jnp.float32).astype(jnp.bfloat16)
            partial_value = lax.optimization_barrier(partial_value)
            total = total + partial_value.astype(jnp.float32)
        return total.astype(jnp.bfloat16)
    return lax.map(block_out, block_ids).reshape(TOKENS, D)
```

```python
import functools

import jax
import jax.numpy as jnp
from jax import lax
from jax.experimental import pallas as pl
from jax.experimental.pallas import tpu as pltpu
from jax.sharding import PartitionSpec as P

SPAN = 64
EPS = 1e-06
BF = jnp.bfloat16
F32 = jnp.float32


def mm(a, b):
    return jnp.dot(a.astype(BF), b.astype(BF), preferred_element_type=F32)


def mm_nt(a, b):
    return lax.dot_general(
        a.astype(BF), b.astype(BF), (((1,), (1,)), ((), ())), preferred_element_type=F32
    )


def mm_tn(a, b):
    return lax.dot_general(
        a.astype(BF), b.astype(BF), (((0,), (0,)), ((), ())), preferred_element_type=F32
    )


def normalize(vector):
    return vector * lax.rsqrt(jnp.sum(vector * vector, axis=-1, keepdims=True) + EPS)


def prefix_sum(rows):
    lane = lax.broadcasted_iota(jnp.int32, rows.shape, 1)
    reach = 1
    while reach < rows.shape[1]:
        rows = rows + jnp.where(lane >= reach, pltpu.roll(rows, reach, 1), 0.0)
        reach *= 2
    return rows


def document_ids(doc_ref, shape, dim):
    span = lax.broadcasted_iota(jnp.int32, shape, dim) // SPAN
    ids = jnp.zeros(shape, jnp.int32)
    for c in range(doc_ref.shape[0]):
        ids = ids + jnp.where(span >= c, doc_ref[c], 0)
    return ids


def fill_bias(doc_ref, bias_ref):
    tokens = bias_ref.shape[0]
    ids_col = document_ids(doc_ref, (tokens, 1), 0)
    ids_row = document_ids(doc_ref, (1, tokens), 1)
    rows = lax.broadcasted_iota(jnp.int32, (tokens, tokens), 0)
    cols = lax.broadcasted_iota(jnp.int32, (tokens, tokens), 1)
    valid = (rows >= cols) & (ids_col == ids_row)
    bias_ref[...] = jnp.where(valid, 0.0, -1e30)


def columns_of(rows):
    count, tokens = rows[0].shape[0] * len(rows), rows[0].shape[1]
    pad = -count % 8
    if pad:
        rows = rows + [jnp.zeros((pad, tokens), F32)]
    return jnp.concatenate(rows, axis=0).T


def unit_lower_inverse(lower):
    size = lower.shape[0]
    rows = lax.broadcasted_iota(jnp.int32, (size, size), 0)
    cols = lax.broadcasted_iota(jnp.int32, (size, size), 1)
    apart = rows ^ cols
    eye = jnp.where(apart == 0, 1.0, 0.0)
    base = 16
    power = jnp.where((apart < base) & (apart > 0), lower, 0.0)
    inverse = eye - power
    reach = 2
    while reach < base:
        power = mm(power, power)
        inverse = inverse + mm(inverse, power)
        reach *= 2
    while base < size:
        off = jnp.where((apart >= base) & (apart < 2 * base), lower, 0.0)
        inverse = inverse - mm(mm(inverse, off), inverse)
        base *= 2
    return inverse


def summary_kernel(
    heads_step, doc_ref, k_ref, v_ref, log_ref, beta_ref, map_ref, inv_ref, erase_ref, bias_ref, cum_ref
):
    tokens = k_ref.shape[0]
    half = tokens // 2
    step = pl.program_id(0)

    @pl.when(step == 0)
    def _():
        fill_bias(doc_ref, bias_ref)
        cum_ref[...] = prefix_sum(log_ref[...])

    ids_col = document_ids(doc_ref, (tokens, 1), 0)
    first = ids_col == 0
    last = ids_col == jnp.max(ids_col)
    hd = 128
    eye = jnp.where(
        lax.broadcasted_iota(jnp.int32, (hd, hd), 0) == lax.broadcasted_iota(jnp.int32, (hd, hd), 1),
        1.0,
        0.0,
    )
    for j in range(heads_step):
        h = step * heads_step + j
        cols = slice(j * hd, (j + 1) * hd)
        key = normalize(k_ref[:, cols].astype(F32))
        key_b = key.astype(BF)
        cum_row = cum_ref[pl.ds(h, 1), :]
        side = columns_of([cum_row, beta_ref[pl.ds(h, 1), :]])
        cum, beta = side[:, 0:1], side[:, 1:2]
        gamma = jnp.where(first, jnp.exp(cum), 0.0)
        total = cum_row[:, tokens - 1 : tokens]
        tail = jnp.where(last, jnp.exp(total - cum), 0.0)

        def lower(r, c):
            rs, cs = slice(r * half, (r + 1) * half), slice(c * half, (c + 1) * half)
            ratio = jnp.exp(cum[rs] - cum_row[:, cs] + bias_ref[rs, cs])
            return ratio * mm_nt(key_b[rs], key_b[cs]) * beta[rs]

        inv0 = unit_lower_inverse(lower(0, 0)).astype(BF)
        inv1 = unit_lower_inverse(lower(1, 1)).astype(BF)
        inv10 = -mm(mm(inv1, lower(1, 0)), inv0)
        inv10 = inv10.astype(BF)
        inv_ref[j, 0] = inv0
        inv_ref[j, 1] = inv10
        inv_ref[j, 2] = inv1
        rhs = jnp.concatenate(
            [beta * v_ref[:, cols].astype(F32), (beta * gamma) * key], axis=1
        ).astype(BF)
        solved0 = mm(inv0, rhs[:half])
        solved1 = mm(inv10, rhs[:half]) + mm(inv1, rhs[half:])
        solved = jnp.concatenate([solved0, solved1], axis=0).astype(BF)
        erase_ref[:, cols] = solved[:, hd:]
        out = mm_tn(tail * key, solved)
        map_ref[0, j] = (gamma[tokens - 1 : tokens, :] * eye - out[:, hd:]).astype(BF)
        map_ref[1, j] = out[:, :hd].astype(BF)


def local_kernel(
    heads_step, doc_ref, q_ref, k_ref, v_ref, log_ref, beta_ref, w_ref, inv_ref, erase_ref,
    y_ref, reader_ref, bias_ref, cum_ref,
):
    tokens = k_ref.shape[0]
    half = tokens // 2
    quarter = half // 2
    step = pl.program_id(0)

    @pl.when(step == 0)
    def _():
        fill_bias(doc_ref, bias_ref)
        cum_ref[...] = prefix_sum(log_ref[...])

    first = document_ids(doc_ref, (tokens, 1), 0) == 0
    hd = 128
    rows = lax.broadcasted_iota(jnp.int32, (quarter, quarter), 0)
    cols_i = lax.broadcasted_iota(jnp.int32, (quarter, quarter), 1)
    same_span = (rows ^ cols_i) < SPAN
    for j in range(heads_step):
        h = step * heads_step + j
        cols = slice(j * hd, (j + 1) * hd)
        key_b = normalize(k_ref[:, cols].astype(F32)).astype(BF)
        query = normalize(q_ref[:, cols].astype(F32))
        query_b = query.astype(BF)
        cum_row = cum_ref[pl.ds(h, 1), :]
        side = columns_of(
            [cum_row, beta_ref[pl.ds(h, 1), :]] + [w_ref[l, pl.ds(h, 1), :] for l in range(4)]
        )
        cum, beta = side[:, 0:1], side[:, 1:2]
        weights = [side[:, 2 + l : 3 + l] for l in range(4)]
        gamma = jnp.where(first, jnp.exp(cum), 0.0)

        def scores(r, c):
            rs, cs = slice(r * half, (r + 1) * half), slice(c * half, (c + 1) * half)
            ratio = jnp.exp(cum[rs] - cum_row[:, cs] + bias_ref[rs, cs])
            return (ratio * mm_nt(query_b[rs], key_b[cs])).astype(BF)

        def within(block, r):
            lo = r * half
            mid = lo + quarter
            a = block[:quarter, :quarter]
            a = a * jnp.where(same_span, weights[0][lo:mid], weights[1][lo:mid])
            b = block[quarter:, :quarter] * weights[2][mid : mid + quarter]
            c = block[quarter:, quarter:]
            c = c * jnp.where(
                same_span, weights[0][mid : mid + quarter], weights[1][mid : mid + quarter]
            )
            top = jnp.concatenate([a, jnp.zeros_like(a)], axis=1)
            return jnp.concatenate([top, jnp.concatenate([b, c], axis=1)], axis=0)

        s00, s10, s11 = scores(0, 0), scores(1, 0), scores(1, 1)
        inv0, inv10, inv1 = inv_ref[j, 0], inv_ref[j, 1], inv_ref[j, 2]
        r00 = within(mm(s00, inv0), 0)
        r11 = within(mm(s11, inv1), 1)
        r10 = (mm(s10, inv0) + mm(s11, inv10)) * weights[3][half:]
        value = (beta * v_ref[:, cols].astype(F32)).astype(BF)
        y_ref[:half, cols] = mm(r00, value[:half])
        y_ref[half:, cols] = mm(r10, value[:half]) + mm(r11, value[half:])
        erase = erase_ref[:, cols]
        reader_ref[:half, cols] = (gamma[:half] * query[:half] - mm(s00, erase[:half])).astype(BF)
        reader_ref[half:, cols] = (
            gamma[half:] * query[half:] - mm(s10, erase[:half]) - mm(s11, erase[half:])
        ).astype(BF)


def finish_kernel(heads_step, low, y_ref, reader_ref, state_ref, w_ref, gain_ref, z_ref):
    step = pl.program_id(0)
    hd = 128
    levels = state_ref.shape[0]
    for j in range(heads_step):
        h = step * heads_step + j
        cols = slice(j * hd, (j + 1) * hd)
        side = columns_of([w_ref[low + l, pl.ds(h, 1), :] for l in range(levels)])
        y = y_ref[:, cols]
        reader = reader_ref[:, cols]
        for l in range(levels):
            y = y + side[:, l : l + 1] * mm(reader, state_ref[l, j])
        y = y * lax.rsqrt(jnp.mean(y * y, axis=-1, keepdims=True) + EPS)
        z_ref[:, cols] = (y * gain_ref[:, cols]).astype(BF)


def from_partner(value, axis, distance):
    return lax.ppermute(value, axis, [(i, i ^ 1 << distance) for i in range(lax.axis_size(axis))])


def bmm(a, b):
    return jnp.einsum("hde,hef->hdf", a, b, preferred_element_type=F32)


def body(queries, keys, values, log_decay, beta, level_weights, doc_start, norm_gain, out_weight):
    tokens = queries.shape[0]
    heads = log_decay.shape[0]
    hd = queries.shape[1] // heads
    half = tokens // 2
    hs = 2
    low = (tokens // SPAN).bit_length()
    grid = (heads // hs,)
    smem = pl.BlockSpec(memory_space=pltpu.SMEM)
    wide = pl.BlockSpec((tokens, hs * hd), lambda i: (0, i))
    whole = pl.BlockSpec((heads, tokens), lambda i: (0, 0))
    level_block = pl.BlockSpec(level_weights.shape, lambda i: (0, 0, 0))
    inv_block = pl.BlockSpec((hs, 3, half, half), lambda i: (i, 0, 0, 0))
    map_block = pl.BlockSpec((2, hs, hd, hd), lambda i: (0, i, 0, 0))
    params = pltpu.CompilerParams(vmem_limit_bytes=48 * 2**20)
    scratch = [pltpu.VMEM((tokens, tokens), F32), pltpu.VMEM((heads, tokens), F32)]
    maps, inv, erase = pl.pallas_call(
        functools.partial(summary_kernel, hs),
        grid=grid,
        out_shape=(
            jax.ShapeDtypeStruct((2, heads, hd, hd), BF),
            jax.ShapeDtypeStruct((heads, 3, half, half), BF),
            jax.ShapeDtypeStruct((tokens, heads * hd), BF),
        ),
        in_specs=[smem, wide, wide, whole, whole],
        out_specs=(map_block, inv_block, wide),
        scratch_shapes=scratch,
        compiler_params=params,
        name="summary",
    )(doc_start, keys, values, log_decay, beta)

    y_local, reader = pl.pallas_call(
        functools.partial(local_kernel, hs),
        grid=grid,
        out_shape=(
            jax.ShapeDtypeStruct((tokens, heads * hd), F32),
            jax.ShapeDtypeStruct((tokens, heads * hd), BF),
        ),
        in_specs=[smem, wide, wide, wide, whole, whole, level_block, inv_block, wide],
        out_specs=(wide, wide),
        scratch_shapes=scratch,
        compiler_params=params,
        cost_estimate=pl.CostEstimate(flops=4 * 10**9, bytes_accessed=12 * 10**6, transcendentals=0),
        name="local",
    )(doc_start, queries, keys, values, log_decay, beta, level_weights, inv, erase)

    nbits = lax.axis_size("seq").bit_length() - 1
    block_idx = lax.axis_index("seq")
    current = maps
    carried = None
    states = []
    for bit in range(nbits):
        sibling = from_partner(current, "seq", bit)
        upper = block_idx >> bit & 1 == 1
        if carried is None:
            reached = sibling.astype(F32)
        else:
            both = jnp.concatenate([sibling[0], sibling[1]], axis=-1)
            reached = bmm(carried.astype(BF), both)
            reached = jnp.stack([reached[..., :hd], reached[..., hd:]])
        states.append(jnp.where(upper, reached[1], 0.0).astype(BF))
        if bit < nbits - 1:
            idle = jnp.broadcast_to(jnp.eye(hd, dtype=F32), (heads, hd, hd)) if bit == 0 else carried
            carried = jnp.where(upper, reached[0], idle)
            first = jnp.where(upper, sibling, current)
            second = jnp.where(upper, current, sibling)
            both = jnp.concatenate([first[0], first[1]], axis=-1)
            merged = bmm(second[0], both)
            current = jnp.stack(
                [merged[..., :hd], merged[..., hd:] + second[1].astype(F32)]
            ).astype(BF)
    states = jnp.stack(states)

    normed = pl.pallas_call(
        functools.partial(finish_kernel, hs, low),
        grid=grid,
        out_shape=jax.ShapeDtypeStruct((tokens, heads * hd), BF),
        in_specs=[
            wide,
            wide,
            pl.BlockSpec((nbits, hs, hd, hd), lambda i: (0, i, 0, 0)),
            level_block,
            pl.BlockSpec((1, hs * hd), lambda i: (0, i)),
        ],
        out_specs=wide,
        compiler_params=params,
        name="finish",
    )(y_local, reader, states, level_weights, norm_gain.reshape(1, -1))
    return lax.psum_scatter(
        jnp.dot(normed, out_weight, preferred_element_type=F32).astype(BF),
        "head",
        scatter_dimension=0,
        tiled=True,
    )


def solution(mesh):
    placed = (
        P("seq", "head"),
        P("seq", "head"),
        P("seq", "head"),
        P("head", "seq"),
        P("head", "seq"),
        P(None, "head", "seq"),
        P("seq"),
        P("head"),
        P("head", None),
    )
    return jax.shard_map(
        body, mesh=mesh, in_specs=placed, out_specs=P(("seq", "head"), None), check_vma=False
    )
```

```python
import functools

import jax
import jax.numpy as jnp
from jax import lax
from jax.experimental import pallas as pl
from jax.experimental.pallas import tpu as pltpu
from jax.sharding import PartitionSpec as P

SPAN = 64
EPS = 1e-06
BF = jnp.bfloat16
F32 = jnp.float32


def mm(a, b):
    return jnp.dot(a.astype(BF), b.astype(BF), preferred_element_type=F32)


def mm_nt(a, b):
    return lax.dot_general(
        a.astype(BF), b.astype(BF), (((1,), (1,)), ((), ())), preferred_element_type=F32
    )


def mm_tn(a, b):
    return lax.dot_general(
        a.astype(BF), b.astype(BF), (((0,), (0,)), ((), ())), preferred_element_type=F32
    )


def normalize(vector):
    return vector * lax.rsqrt(jnp.sum(vector * vector, axis=-1, keepdims=True) + EPS)


def prefix_sum(rows):
    lane = lax.broadcasted_iota(jnp.int32, rows.shape, 1)
    reach = 1
    while reach < rows.shape[1]:
        rows = rows + jnp.where(lane >= reach, pltpu.roll(rows, reach, 1), 0.0)
        reach *= 2
    return rows


def document_ids(doc_ref, shape, dim):
    span = lax.broadcasted_iota(jnp.int32, shape, dim) // SPAN
    ids = jnp.zeros(shape, jnp.int32)
    for c in range(doc_ref.shape[0]):
        ids = ids + jnp.where(span >= c, doc_ref[c], 0)
    return ids


def fill_bias(doc_ref, bias_ref):
    tokens = bias_ref.shape[0]
    ids_col = document_ids(doc_ref, (tokens, 1), 0)
    ids_row = document_ids(doc_ref, (1, tokens), 1)
    rows = lax.broadcasted_iota(jnp.int32, (tokens, tokens), 0)
    cols = lax.broadcasted_iota(jnp.int32, (tokens, tokens), 1)
    valid = (rows >= cols) & (ids_col == ids_row)
    bias_ref[...] = jnp.where(valid, 0.0, -1e30)


def columns_of(rows):
    count, tokens = rows[0].shape[0] * len(rows), rows[0].shape[1]
    pad = -count % 8
    if pad:
        rows = rows + [jnp.zeros((pad, tokens), F32)]
    return jnp.concatenate(rows, axis=0).T


def unit_lower_inverses(lowers):
    size = lowers[0].shape[0]
    rows = lax.broadcasted_iota(jnp.int32, (size, size), 0)
    cols = lax.broadcasted_iota(jnp.int32, (size, size), 1)
    apart = rows ^ cols
    eye = jnp.where(apart == 0, 1.0, 0.0)
    base = 16
    inside = (apart < base) & (apart > 0)
    powers = [jnp.where(inside, lower, 0.0) for lower in lowers]
    inverses = [eye - power for power in powers]
    powers = [mm(power, power) for power in powers]
    reach = 2
    while reach < base:
        if 2 * reach < base:
            both = [
                mm(jnp.concatenate([power.astype(BF), inverse.astype(BF)], axis=0), power)
                for power, inverse in zip(powers, inverses)
            ]
            powers = [pair[:size] for pair in both]
            inverses = [inverse + pair[size:] for inverse, pair in zip(inverses, both)]
        else:
            inverses = [inverse + mm(inverse, power) for power, inverse in zip(powers, inverses)]
        reach *= 2
    while base < size:
        band = (apart >= base) & (apart < 2 * base)
        offs = [jnp.where(band, lower, 0.0).astype(BF) for lower in lowers]
        held = [inverse.astype(BF) for inverse in inverses]
        steps = [mm(inverse, off) for inverse, off in zip(held, offs)]
        steps = [mm(first, inverse) for first, inverse in zip(steps, held)]
        inverses = [inverse - step for inverse, step in zip(inverses, steps)]
        base *= 2
    return [inverse.astype(BF) for inverse in inverses]


def summary_kernel(
    heads_step, doc_ref, k_ref, v_ref, log_ref, beta_ref, map_ref, inv_ref, erase_ref, bias_ref, cum_ref
):
    tokens = k_ref.shape[0]
    half = tokens // 2
    step = pl.program_id(0)

    @pl.when(step == 0)
    def _():
        fill_bias(doc_ref, bias_ref)
        cum_ref[...] = prefix_sum(log_ref[...])

    ids_col = document_ids(doc_ref, (tokens, 1), 0)
    first_doc = ids_col == 0
    last_doc = ids_col == jnp.max(ids_col)
    hd = 128
    eye = jnp.where(
        lax.broadcasted_iota(jnp.int32, (hd, hd), 0) == lax.broadcasted_iota(jnp.int32, (hd, hd), 1),
        1.0,
        0.0,
    )
    heads = range(heads_step)
    col_of = [slice(j * hd, (j + 1) * hd) for j in heads]
    keys = [normalize(k_ref[:, c].astype(F32)) for c in col_of]
    keys_b = [key.astype(BF) for key in keys]
    cum_rows = [cum_ref[pl.ds(step * heads_step + j, 1), :] for j in heads]
    sides = [
        columns_of([cum_rows[j], beta_ref[pl.ds(step * heads_step + j, 1), :]]) for j in heads
    ]
    cums, betas = [side[:, 0:1] for side in sides], [side[:, 1:2] for side in sides]
    quarter = half // 2
    parts = tokens // quarter

    def lower(j, rs, cs):
        ratio = jnp.exp(cums[j][rs] - cum_rows[j][:, cs] + bias_ref[rs, cs])
        return ratio * mm_nt(keys_b[j][rs], keys_b[j][cs]) * betas[j][rs]

    piece = [slice(i * quarter, (i + 1) * quarter) for i in range(parts)]
    diagonal = unit_lower_inverses([lower(j, p, p) for j in heads for p in piece])
    merges = [(j, i) for j in heads for i in range(0, parts, 2)]
    firsts = [
        mm(diagonal[j * parts + i + 1], lower(j, piece[i + 1], piece[i])) for j, i in merges
    ]
    corners = [
        -mm(first, diagonal[j * parts + i]) for first, (j, i) in zip(firsts, merges)
    ]
    inverses = []
    for corner, (j, i) in zip(corners, merges):
        a, b = diagonal[j * parts + i], diagonal[j * parts + i + 1]
        top = jnp.concatenate([a, jnp.zeros_like(a)], axis=1)
        inverses.append(
            jnp.concatenate([top, jnp.concatenate([corner.astype(BF), b], axis=1)], axis=0)
        )
    low, high = slice(0, half), slice(half, tokens)
    firsts = [mm(inverses[2 * j + 1], lower(j, high, low)) for j in heads]
    cross = [(-mm(first, inverses[2 * j])).astype(BF) for j, first in enumerate(firsts)]
    for j in heads:
        c, key, cum, beta = col_of[j], keys[j], cums[j], betas[j]
        inv0, inv10, inv1 = inverses[2 * j], cross[j], inverses[2 * j + 1]
        inv_ref[j, 0] = inv0
        inv_ref[j, 1] = inv10
        inv_ref[j, 2] = inv1
        gamma = jnp.where(first_doc, jnp.exp(cum), 0.0)
        tail = jnp.where(last_doc, jnp.exp(cum_rows[j][:, tokens - 1 : tokens] - cum), 0.0)
        rhs = jnp.concatenate(
            [beta * v_ref[:, c].astype(F32), (beta * gamma) * key], axis=1
        ).astype(BF)
        solved0 = mm(inv0, rhs[:half])
        solved1 = mm(inv10, rhs[:half]) + mm(inv1, rhs[half:])
        solved = jnp.concatenate([solved0, solved1], axis=0).astype(BF)
        erase_ref[:, c] = solved[:, hd:]
        out = mm_tn(tail * key, solved)
        map_ref[0, j] = (gamma[tokens - 1 : tokens, :] * eye - out[:, hd:]).astype(BF)
        map_ref[1, j] = out[:, :hd].astype(BF)


def local_kernel(
    heads_step, doc_ref, q_ref, k_ref, v_ref, log_ref, beta_ref, w_ref, inv_ref, erase_ref,
    y_ref, reader_ref, bias_ref, cum_ref,
):
    tokens = k_ref.shape[0]
    half = tokens // 2
    quarter = half // 2
    step = pl.program_id(0)

    @pl.when(step == 0)
    def _():
        fill_bias(doc_ref, bias_ref)
        cum_ref[...] = prefix_sum(log_ref[...])

    first = document_ids(doc_ref, (tokens, 1), 0) == 0
    hd = 128
    rows = lax.broadcasted_iota(jnp.int32, (quarter, quarter), 0)
    cols_i = lax.broadcasted_iota(jnp.int32, (quarter, quarter), 1)
    same_span = (rows ^ cols_i) < SPAN
    for j in range(heads_step):
        h = step * heads_step + j
        cols = slice(j * hd, (j + 1) * hd)
        key_b = normalize(k_ref[:, cols].astype(F32)).astype(BF)
        query = normalize(q_ref[:, cols].astype(F32))
        query_b = query.astype(BF)
        cum_row = cum_ref[pl.ds(h, 1), :]
        side = columns_of(
            [cum_row, beta_ref[pl.ds(h, 1), :]] + [w_ref[l, pl.ds(h, 1), :] for l in range(4)]
        )
        cum, beta = side[:, 0:1], side[:, 1:2]
        weights = [side[:, 2 + l : 3 + l] for l in range(4)]
        gamma = jnp.where(first, jnp.exp(cum), 0.0)

        def scores(r, c):
            rs, cs = slice(r * half, (r + 1) * half), slice(c * half, (c + 1) * half)
            ratio = jnp.exp(cum[rs] - cum_row[:, cs] + bias_ref[rs, cs])
            return (ratio * mm_nt(query_b[rs], key_b[cs])).astype(BF)

        def within(block, r):
            lo = r * half
            mid = lo + quarter
            a = block[:quarter, :quarter]
            a = a * jnp.where(same_span, weights[0][lo:mid], weights[1][lo:mid])
            b = block[quarter:, :quarter] * weights[2][mid : mid + quarter]
            c = block[quarter:, quarter:]
            c = c * jnp.where(
                same_span, weights[0][mid : mid + quarter], weights[1][mid : mid + quarter]
            )
            top = jnp.concatenate([a, jnp.zeros_like(a)], axis=1)
            return jnp.concatenate([top, jnp.concatenate([b, c], axis=1)], axis=0)

        s00, s10, s11 = scores(0, 0), scores(1, 0), scores(1, 1)
        inv0, inv10, inv1 = inv_ref[j, 0], inv_ref[j, 1], inv_ref[j, 2]
        r00 = within(mm(s00, inv0), 0)
        r11 = within(mm(s11, inv1), 1)
        r10 = (mm(s10, inv0) + mm(s11, inv10)) * weights[3][half:]
        value = (beta * v_ref[:, cols].astype(F32)).astype(BF)
        y_ref[:half, cols] = mm(r00, value[:half])
        y_ref[half:, cols] = mm(r10, value[:half]) + mm(r11, value[half:])
        erase = erase_ref[:, cols]
        reader_ref[:half, cols] = (gamma[:half] * query[:half] - mm(s00, erase[:half])).astype(BF)
        reader_ref[half:, cols] = (
            gamma[half:] * query[half:] - mm(s10, erase[:half]) - mm(s11, erase[half:])
        ).astype(BF)


def finish_kernel(heads_step, low, y_ref, reader_ref, state_ref, w_ref, gain_ref, z_ref):
    step = pl.program_id(0)
    hd = 128
    levels = state_ref.shape[0]
    for j in range(heads_step):
        h = step * heads_step + j
        cols = slice(j * hd, (j + 1) * hd)
        side = columns_of([w_ref[low + l, pl.ds(h, 1), :] for l in range(levels)])
        y = y_ref[:, cols]
        reader = reader_ref[:, cols]
        for l in range(levels):
            y = y + side[:, l : l + 1] * mm(reader, state_ref[l, j])
        y = y * lax.rsqrt(jnp.mean(y * y, axis=-1, keepdims=True) + EPS)
        z_ref[:, cols] = (y * gain_ref[:, cols]).astype(BF)


def project_kernel(
    chunk, z_ref, w_hbm, out_ref, w_ref, keep, send_a, recv_a, send_y, recv_y, send_b, recv_b,
    w_sem, sa_sem, ra_sem, sy_sem, ry_sem, sb_sem, rb_sem,
):
    me = lax.axis_index("head")
    mate = me + 1 - 2 * (me % 2)
    across = (me + 2) % 4
    far_mate = (mate + 2) % 4
    count = keep.shape[1]
    rows = keep.shape[2]

    def columns(j):
        return pl.ds(pl.multiple_of(j * chunk, chunk), chunk)

    def load(j):
        return pltpu.make_async_copy(w_hbm.at[:, columns(j)], w_ref.at[:, columns(j)], w_sem.at[j])

    def remote(src, dst, ssem, rsem, j, target):
        return pltpu.make_async_remote_copy(
            src_ref=src.at[j],
            dst_ref=dst.at[j],
            send_sem=ssem.at[j],
            recv_sem=rsem.at[j],
            device_id={"head": target},
            device_id_type=pl.DeviceIdType.MESH,
        )

    def copy_a(j):
        return remote(send_a, recv_a, sa_sem, ra_sem, j, mate)

    def copy_b(j):
        return remote(send_b, recv_b, sb_sem, rb_sem, j, mate)

    def copy_y(j):
        return remote(send_y, recv_y, sy_sem, ry_sem, j, across)

    def block(owner):
        return z_ref[pl.ds(pl.multiple_of(owner * rows, rows), rows), :]

    lax.fori_loop(0, count, lambda j, _: (load(j).start(), 0)[1], 0)
    barrier = pltpu.get_barrier_semaphore()
    for other in (mate, across):
        pl.semaphore_signal(
            barrier, inc=1, device_id={"head": other}, device_id_type=pl.DeviceIdType.MESH
        )
    pl.semaphore_wait(barrier, 2)

    def forward(j):
        copy_a(j).wait_recv()
        send_y[j] = (keep[0, j] + recv_a[j].astype(F32)).astype(BF)
        copy_y(j).start()

    def far(j, _):
        load(j).wait()
        weight = w_ref[:, columns(j)]
        send_a[j] = jnp.dot(block(far_mate), weight, preferred_element_type=F32).astype(BF)
        copy_a(j).start()
        keep[0, j] = jnp.dot(block(across), weight, preferred_element_type=F32)

        @pl.when(j > 0)
        def _():
            forward(j - 1)

        return 0

    lax.fori_loop(0, count, far, 0)
    forward(count - 1)

    def near(j, _):
        weight = w_ref[:, columns(j)]
        send_b[j] = jnp.dot(block(mate), weight, preferred_element_type=F32).astype(BF)
        copy_b(j).start()
        keep[1, j] = jnp.dot(block(me), weight, preferred_element_type=F32)
        return 0

    lax.fori_loop(0, count, near, 0)

    def close(j, _):
        copy_b(j).wait_recv()
        copy_y(j).wait_recv()
        total = keep[1, j] + recv_b[j].astype(F32) + recv_y[j].astype(F32)
        out_ref[:, columns(j)] = total.astype(BF)
        copy_a(j).wait_send()
        copy_b(j).wait_send()
        copy_y(j).wait_send()
        return 0

    lax.fori_loop(0, count, close, 0)


def project(normed, out_weight):
    tokens, width = normed.shape
    out_width = out_weight.shape[1]
    rows = tokens // 4
    chunk = min(512, out_width)
    count = out_width // chunk
    slab = pltpu.VMEM((count, rows, chunk), BF)
    sems = [pltpu.SemaphoreType.DMA((count,))] * 7
    return pl.pallas_call(
        functools.partial(project_kernel, chunk),
        out_shape=jax.ShapeDtypeStruct((rows, out_width), BF),
        in_specs=[pl.BlockSpec(memory_space=pltpu.VMEM), pl.BlockSpec(memory_space=pl.ANY)],
        out_specs=pl.BlockSpec(memory_space=pltpu.VMEM),
        scratch_shapes=[
            pltpu.VMEM((width, out_width), BF),
            pltpu.VMEM((2, count, rows, chunk), F32),
        ]
        + [slab] * 6
        + sems,
        compiler_params=pltpu.CompilerParams(
            collective_id=0, has_side_effects=True, vmem_limit_bytes=56 * 2**20
        ),
        name="project",
    )(normed, out_weight)


def from_partner(value, axis, distance):
    return lax.ppermute(value, axis, [(i, i ^ 1 << distance) for i in range(lax.axis_size(axis))])


def bmm(a, b):
    return jnp.einsum("hde,hef->hdf", a, b, preferred_element_type=F32)


def body(queries, keys, values, log_decay, beta, level_weights, doc_start, norm_gain, out_weight):
    tokens = queries.shape[0]
    heads = log_decay.shape[0]
    hd = queries.shape[1] // heads
    half = tokens // 2
    hs = 2
    low = (tokens // SPAN).bit_length()
    grid = (heads // hs,)
    smem = pl.BlockSpec(memory_space=pltpu.SMEM)
    wide = pl.BlockSpec((tokens, hs * hd), lambda i: (0, i))
    whole = pl.BlockSpec((heads, tokens), lambda i: (0, 0))
    level_block = pl.BlockSpec(level_weights.shape, lambda i: (0, 0, 0))
    inv_block = pl.BlockSpec((hs, 3, half, half), lambda i: (i, 0, 0, 0))
    map_block = pl.BlockSpec((2, hs, hd, hd), lambda i: (0, i, 0, 0))
    params = pltpu.CompilerParams(vmem_limit_bytes=56 * 2**20)
    scratch = [pltpu.VMEM((tokens, tokens), F32), pltpu.VMEM((heads, tokens), F32)]
    maps, inv, erase = pl.pallas_call(
        functools.partial(summary_kernel, hs),
        grid=grid,
        out_shape=(
            jax.ShapeDtypeStruct((2, heads, hd, hd), BF),
            jax.ShapeDtypeStruct((heads, 3, half, half), BF),
            jax.ShapeDtypeStruct((tokens, heads * hd), BF),
        ),
        in_specs=[smem, wide, wide, whole, whole],
        out_specs=(map_block, inv_block, wide),
        scratch_shapes=scratch,
        compiler_params=params,
        name="summary",
    )(doc_start, keys, values, log_decay, beta)

    y_local, reader = pl.pallas_call(
        functools.partial(local_kernel, hs),
        grid=grid,
        out_shape=(
            jax.ShapeDtypeStruct((tokens, heads * hd), F32),
            jax.ShapeDtypeStruct((tokens, heads * hd), BF),
        ),
        in_specs=[smem, wide, wide, wide, whole, whole, level_block, inv_block, wide],
        out_specs=(wide, wide),
        scratch_shapes=scratch,
        compiler_params=params,
        cost_estimate=pl.CostEstimate(flops=4 * 10**9, bytes_accessed=12 * 10**6, transcendentals=0),
        name="local",
    )(doc_start, queries, keys, values, log_decay, beta, level_weights, inv, erase)

    nbits = lax.axis_size("seq").bit_length() - 1
    block_idx = lax.axis_index("seq")
    current = maps
    carried = None
    states = []
    for bit in range(nbits):
        sibling = from_partner(current, "seq", bit)
        upper = block_idx >> bit & 1 == 1
        if carried is None:
            reached = sibling.astype(F32)
        else:
            both = jnp.concatenate([sibling[0], sibling[1]], axis=-1)
            reached = bmm(carried.astype(BF), both)
            reached = jnp.stack([reached[..., :hd], reached[..., hd:]])
        states.append(jnp.where(upper, reached[1], 0.0).astype(BF))
        if bit < nbits - 1:
            idle = jnp.broadcast_to(jnp.eye(hd, dtype=F32), (heads, hd, hd)) if bit == 0 else carried
            carried = jnp.where(upper, reached[0], idle)
            first = jnp.where(upper, sibling, current)
            second = jnp.where(upper, current, sibling)
            both = jnp.concatenate([first[0], first[1]], axis=-1)
            merged = bmm(second[0], both)
            current = jnp.stack(
                [merged[..., :hd], merged[..., hd:] + second[1].astype(F32)]
            ).astype(BF)
    states = jnp.stack(states)

    normed = pl.pallas_call(
        functools.partial(finish_kernel, hs, low),
        grid=grid,
        out_shape=jax.ShapeDtypeStruct((tokens, heads * hd), BF),
        in_specs=[
            wide,
            wide,
            pl.BlockSpec((nbits, hs, hd, hd), lambda i: (0, i, 0, 0)),
            level_block,
            pl.BlockSpec((1, hs * hd), lambda i: (0, i)),
        ],
        out_specs=wide,
        compiler_params=params,
        name="finish",
    )(y_local, reader, states, level_weights, norm_gain.reshape(1, -1))
    return project(normed, out_weight)


def solution(mesh):
    placed = (
        P("seq", "head"),
        P("seq", "head"),
        P("seq", "head"),
        P("head", "seq"),
        P("head", "seq"),
        P(None, "head", "seq"),
        P("seq"),
        P("head"),
        P("head", None),
    )
    return jax.shard_map(
        body, mesh=mesh, in_specs=placed, out_specs=P(("seq", "head"), None), check_vma=False
    )
```

```python
import functools

import jax
import jax.numpy as jnp
from jax import lax
from jax.experimental import pallas as pl
from jax.experimental.pallas import tpu as pltpu
from jax.sharding import PartitionSpec as P

SPAN = 64
EPS = 1e-06
BF = jnp.bfloat16
F32 = jnp.float32


def mm(a, b):
    return jnp.dot(a.astype(BF), b.astype(BF), preferred_element_type=F32)


def mm_nt(a, b):
    return lax.dot_general(
        a.astype(BF), b.astype(BF), (((1,), (1,)), ((), ())), preferred_element_type=F32
    )


def mm_tn(a, b):
    return lax.dot_general(
        a.astype(BF), b.astype(BF), (((0,), (0,)), ((), ())), preferred_element_type=F32
    )


def normalize(vector):
    return vector * lax.rsqrt(jnp.sum(vector * vector, axis=-1, keepdims=True) + EPS)


def prefix_sum(rows):
    lane = lax.broadcasted_iota(jnp.int32, rows.shape, 1)
    reach = 1
    while reach < rows.shape[1]:
        rows = rows + jnp.where(lane >= reach, pltpu.roll(rows, reach, 1), 0.0)
        reach *= 2
    return rows


def document_ids(doc_ref, shape, dim):
    span = lax.broadcasted_iota(jnp.int32, shape, dim) // SPAN
    ids = jnp.zeros(shape, jnp.int32)
    for c in range(doc_ref.shape[0]):
        ids = ids + jnp.where(span >= c, doc_ref[c], 0)
    return ids


def fill_bias(doc_ref, bias_ref):
    tokens = bias_ref.shape[0]
    ids_col = document_ids(doc_ref, (tokens, 1), 0)
    ids_row = document_ids(doc_ref, (1, tokens), 1)
    rows = lax.broadcasted_iota(jnp.int32, (tokens, tokens), 0)
    cols = lax.broadcasted_iota(jnp.int32, (tokens, tokens), 1)
    valid = (rows >= cols) & (ids_col == ids_row)
    bias_ref[...] = jnp.where(valid, 0.0, -1e30)


def columns_of(rows):
    count, tokens = rows[0].shape[0] * len(rows), rows[0].shape[1]
    pad = -count % 8
    if pad:
        rows = rows + [jnp.zeros((pad, tokens), F32)]
    return jnp.concatenate(rows, axis=0).T


def unit_lower_inverses(lowers):
    size = lowers[0].shape[0]
    rows = lax.broadcasted_iota(jnp.int32, (size, size), 0)
    cols = lax.broadcasted_iota(jnp.int32, (size, size), 1)
    apart = rows ^ cols
    eye = jnp.where(apart == 0, 1.0, 0.0)
    base = 16
    inside = (apart < base) & (apart > 0)
    powers = [jnp.where(inside, lower, 0.0) for lower in lowers]
    inverses = [eye - power for power in powers]
    powers = [mm(power, power) for power in powers]
    reach = 2
    while reach < base:
        if 2 * reach < base:
            both = [
                mm(jnp.concatenate([power.astype(BF), inverse.astype(BF)], axis=0), power)
                for power, inverse in zip(powers, inverses)
            ]
            powers = [pair[:size] for pair in both]
            inverses = [inverse + pair[size:] for inverse, pair in zip(inverses, both)]
        else:
            inverses = [inverse + mm(inverse, power) for power, inverse in zip(powers, inverses)]
        reach *= 2
    while base < size:
        band = (apart >= base) & (apart < 2 * base)
        offs = [jnp.where(band, lower, 0.0).astype(BF) for lower in lowers]
        held = [inverse.astype(BF) for inverse in inverses]
        steps = [mm(inverse, off) for inverse, off in zip(held, offs)]
        steps = [mm(first, inverse) for first, inverse in zip(steps, held)]
        inverses = [inverse - step for inverse, step in zip(inverses, steps)]
        base *= 2
    return [inverse.astype(BF) for inverse in inverses]


def form_maps(step, heads_step, doc_ref, k_ref, v_ref, beta_ref, inv_ref, erase_ref, map_ref, bias_ref, cum_ref):
    tokens = k_ref.shape[0]
    half = tokens // 2
    ids_col = document_ids(doc_ref, (tokens, 1), 0)
    first_doc = ids_col == 0
    last_doc = ids_col == jnp.max(ids_col)
    hd = 128
    eye = jnp.where(
        lax.broadcasted_iota(jnp.int32, (hd, hd), 0) == lax.broadcasted_iota(jnp.int32, (hd, hd), 1),
        1.0,
        0.0,
    )
    heads = range(heads_step)
    col_of = [slice(j * hd, (j + 1) * hd) for j in heads]
    keys = [normalize(k_ref[:, c].astype(F32)) for c in col_of]
    keys_b = [key.astype(BF) for key in keys]
    cum_rows = [cum_ref[pl.ds(step * heads_step + j, 1), :] for j in heads]
    sides = [
        columns_of([cum_rows[j], beta_ref[pl.ds(step * heads_step + j, 1), :]]) for j in heads
    ]
    cums, betas = [side[:, 0:1] for side in sides], [side[:, 1:2] for side in sides]
    quarter = half // 2
    parts = tokens // quarter

    def lower(j, rs, cs):
        ratio = jnp.exp(cums[j][rs] - cum_rows[j][:, cs] + bias_ref[rs, cs])
        return ratio * mm_nt(keys_b[j][rs], keys_b[j][cs]) * betas[j][rs]

    piece = [slice(i * quarter, (i + 1) * quarter) for i in range(parts)]
    diagonal = unit_lower_inverses([lower(j, p, p) for j in heads for p in piece])
    merges = [(j, i) for j in heads for i in range(0, parts, 2)]
    firsts = [
        mm(diagonal[j * parts + i + 1], lower(j, piece[i + 1], piece[i])) for j, i in merges
    ]
    corners = [
        -mm(first, diagonal[j * parts + i]) for first, (j, i) in zip(firsts, merges)
    ]
    inverses = []
    for corner, (j, i) in zip(corners, merges):
        a, b = diagonal[j * parts + i], diagonal[j * parts + i + 1]
        top = jnp.concatenate([a, jnp.zeros_like(a)], axis=1)
        inverses.append(
            jnp.concatenate([top, jnp.concatenate([corner.astype(BF), b], axis=1)], axis=0)
        )
    low, high = slice(0, half), slice(half, tokens)
    firsts = [mm(inverses[2 * j + 1], lower(j, high, low)) for j in heads]
    cross = [(-mm(first, inverses[2 * j])).astype(BF) for j, first in enumerate(firsts)]
    for j in heads:
        c, key, cum, beta = col_of[j], keys[j], cums[j], betas[j]
        inv0, inv10, inv1 = inverses[2 * j], cross[j], inverses[2 * j + 1]
        inv_ref[step, j, 0] = inv0
        inv_ref[step, j, 1] = inv10
        inv_ref[step, j, 2] = inv1
        gamma = jnp.where(first_doc, jnp.exp(cum), 0.0)
        tail = jnp.where(last_doc, jnp.exp(cum_rows[j][:, tokens - 1 : tokens] - cum), 0.0)
        rhs = jnp.concatenate(
            [beta * v_ref[:, c].astype(F32), (beta * gamma) * key], axis=1
        ).astype(BF)
        solved0 = mm(inv0, rhs[:half])
        solved1 = mm(inv10, rhs[:half]) + mm(inv1, rhs[half:])
        solved = jnp.concatenate([solved0, solved1], axis=0).astype(BF)
        erase_ref[step, :, c] = solved[:, hd:]
        out = mm_tn(tail * key, solved)
        map_ref[0, step, 0, j] = (gamma[tokens - 1 : tokens, :] * eye - out[:, hd:]).astype(BF)
        map_ref[0, step, 1, j] = out[:, :hd].astype(BF)


def read_block(step, heads_step, doc_ref, q_ref, k_ref, v_ref, beta_ref, w_ref, inv_ref, erase_ref, y_ref, reader_ref, bias_ref, cum_ref):
    tokens = k_ref.shape[0]
    half = tokens // 2
    quarter = half // 2
    first = document_ids(doc_ref, (tokens, 1), 0) == 0
    hd = 128
    rows = lax.broadcasted_iota(jnp.int32, (quarter, quarter), 0)
    cols_i = lax.broadcasted_iota(jnp.int32, (quarter, quarter), 1)
    same_span = (rows ^ cols_i) < SPAN
    for j in range(heads_step):
        h = step * heads_step + j
        cols = slice(j * hd, (j + 1) * hd)
        key_b = normalize(k_ref[:, cols].astype(F32)).astype(BF)
        query = normalize(q_ref[:, cols].astype(F32))
        query_b = query.astype(BF)
        cum_row = cum_ref[pl.ds(h, 1), :]
        side = columns_of(
            [cum_row, beta_ref[pl.ds(h, 1), :]] + [w_ref[l, pl.ds(h, 1), :] for l in range(4)]
        )
        cum, beta = side[:, 0:1], side[:, 1:2]
        weights = [side[:, 2 + l : 3 + l] for l in range(4)]
        gamma = jnp.where(first, jnp.exp(cum), 0.0)

        def scores(r, c):
            rs, cs = slice(r * half, (r + 1) * half), slice(c * half, (c + 1) * half)
            ratio = jnp.exp(cum[rs] - cum_row[:, cs] + bias_ref[rs, cs])
            return (ratio * mm_nt(query_b[rs], key_b[cs])).astype(BF)

        def within(block, r):
            lo = r * half
            mid = lo + quarter
            a = block[:quarter, :quarter]
            a = a * jnp.where(same_span, weights[0][lo:mid], weights[1][lo:mid])
            b = block[quarter:, :quarter] * weights[2][mid : mid + quarter]
            c = block[quarter:, quarter:]
            c = c * jnp.where(
                same_span, weights[0][mid : mid + quarter], weights[1][mid : mid + quarter]
            )
            top = jnp.concatenate([a, jnp.zeros_like(a)], axis=1)
            return jnp.concatenate([top, jnp.concatenate([b, c], axis=1)], axis=0)

        s00, s10, s11 = scores(0, 0), scores(1, 0), scores(1, 1)
        inv0, inv10, inv1 = inv_ref[step, j, 0], inv_ref[step, j, 1], inv_ref[step, j, 2]
        r00 = within(mm(s00, inv0), 0)
        r11 = within(mm(s11, inv1), 1)
        r10 = (mm(s10, inv0) + mm(s11, inv10)) * weights[3][half:]
        value = (beta * v_ref[:, cols].astype(F32)).astype(BF)
        y_ref[step, :half, cols] = mm(r00, value[:half])
        y_ref[step, half:, cols] = mm(r10, value[:half]) + mm(r11, value[half:])
        erase = erase_ref[step, :, cols]
        reader_ref[step, :half, cols] = (gamma[:half] * query[:half] - mm(s00, erase[:half])).astype(BF)
        reader_ref[step, half:, cols] = (
            gamma[half:] * query[half:] - mm(s10, erase[:half]) - mm(s11, erase[half:])
        ).astype(BF)


def finish_block(step, heads_step, low, y_ref, reader_ref, state_ref, w_ref, gain_ref, z_ref):
    hd = 128
    levels = state_ref.shape[0]
    for j in range(heads_step):
        h = step * heads_step + j
        cols = slice(j * hd, (j + 1) * hd)
        side = columns_of([w_ref[low + l, pl.ds(h, 1), :] for l in range(levels)])
        y = y_ref[step, :, cols]
        reader = reader_ref[step, :, cols]
        for l in range(levels):
            y = y + side[:, l : l + 1] * mm(reader, state_ref[l, step, j])
        y = y * lax.rsqrt(jnp.mean(y * y, axis=-1, keepdims=True) + EPS)
        z_ref[:, cols] = (y * gain_ref[:, cols]).astype(BF)


def mixer_kernel(
    hs, low, doc_ref, q_ref, k_ref, v_ref, log_ref, beta_ref, w_ref, gain_ref, z_ref,
    bias_ref, cum_ref, inv_ref, erase_ref, y_ref, reader_ref, send, recv, carried, states,
    send_sem, recv_sem,
):
    step = pl.program_id(0)
    nbits, groups = send.shape[0], send.shape[1]
    hd = send.shape[-1]
    block = lax.axis_index("seq")
    barrier = pltpu.get_barrier_semaphore()

    def partner(bit):
        return block + (1 << bit) * (1 - 2 * ((block // (1 << bit)) % 2))

    def copy(bit, g):
        whole = bit < nbits - 1
        return pltpu.make_async_remote_copy(
            src_ref=send.at[bit, g] if whole else send.at[bit, g, 1],
            dst_ref=recv.at[bit, g] if whole else recv.at[bit, g, 1],
            send_sem=send_sem.at[bit, g],
            recv_sem=recv_sem.at[bit, g],
            device_id={"seq": partner(bit)},
            device_id_type=pl.DeviceIdType.MESH,
        )

    @pl.when(step == 0)
    def _():
        for bit in range(nbits):
            pl.semaphore_signal(
                barrier, inc=1, device_id={"seq": partner(bit)}, device_id_type=pl.DeviceIdType.MESH
            )
        fill_bias(doc_ref, bias_ref)
        cum_ref[...] = prefix_sum(log_ref[...])

    @pl.when(step < groups)
    def _():
        form_maps(
            step, hs, doc_ref, k_ref, v_ref, beta_ref, inv_ref, erase_ref, send, bias_ref, cum_ref
        )

    @pl.when(step == 0)
    def _():
        pl.semaphore_wait(barrier, nbits)

    @pl.when(step < groups)
    def _():
        copy(0, step).start()

    @pl.when((step >= groups) & (step < 2 * groups))
    def _():
        read_block(
            step - groups, hs, doc_ref, q_ref, k_ref, v_ref, beta_ref, w_ref, inv_ref, erase_ref,
            y_ref, reader_ref, bias_ref, cum_ref,
        )

    @pl.when(step >= 2 * groups)
    def _():
        finish_block(
            step - 2 * groups, hs, low, y_ref, reader_ref, states, w_ref, gain_ref, z_ref
        )

    def exchange(bit, g):
        copy(bit, g).wait_recv()
        upper = (block // (1 << bit)) % 2 == 1
        eye = jnp.where(
            lax.broadcasted_iota(jnp.int32, (hd, hd), 0)
            == lax.broadcasted_iota(jnp.int32, (hd, hd), 1),
            1.0,
            0.0,
        )
        more = bit < nbits - 1
        for j in range(hs):
            sib_s = recv[bit, g, 1, j]
            if more:
                sib_t = recv[bit, g, 0, j]
            if bit == 0:
                reached_s = sib_s.astype(F32)
                if more:
                    carried[g, j] = jnp.where(upper, sib_t.astype(F32), eye)
            elif more:
                held = carried[g, j]
                both = mm(held, jnp.concatenate([sib_t, sib_s], axis=1))
                reached_s = both[:, hd:]
                carried[g, j] = jnp.where(upper, both[:, :hd], held)
            else:
                reached_s = mm(carried[g, j], sib_s)
            states[bit, g, j] = jnp.where(upper, reached_s, 0.0).astype(BF)
            if more:
                sib = jnp.concatenate([sib_t, sib_s], axis=1).astype(F32)
                own = jnp.concatenate([send[bit, g, 0, j], send[bit, g, 1, j]], axis=1).astype(F32)
                first = jnp.where(upper, sib, own)
                second = jnp.where(upper, own, sib)
                merged = mm(second[:, :hd], first)
                send[bit + 1, g, 0, j] = merged[:, :hd].astype(BF)
                send[bit + 1, g, 1, j] = (merged[:, hd:] + second[:, hd:]).astype(BF)
        if more:
            copy(bit + 1, g).start()

    for bit in range(nbits):
        g = step - 1 - bit

        @pl.when((g >= 0) & (g < groups))
        def _(bit=bit, g=g):
            exchange(bit, g)

    @pl.when(step == 3 * groups - 1)
    def _():
        for bit in range(nbits):
            for g in range(groups):
                copy(bit, g).wait_send()


def mixer(queries, keys, values, log_decay, beta, level_weights, doc_start, norm_gain):
    tokens = queries.shape[0]
    heads = log_decay.shape[0]
    hd = queries.shape[1] // heads
    half = tokens // 2
    hs = 2
    groups = heads // hs
    low = (tokens // SPAN).bit_length()
    nbits = lax.axis_size("seq").bit_length() - 1
    wide = (tokens, hs * hd)

    def both(i):
        return (0, jnp.minimum(i, 2 * groups - 1) % groups)

    def second(i):
        return (0, jnp.clip(i - groups, 0, groups - 1))

    def third(i):
        return (0, jnp.clip(i - 2 * groups, 0, groups - 1))

    row_block = pl.BlockSpec((heads, tokens), lambda i: (0, 0))
    return pl.pallas_call(
        functools.partial(mixer_kernel, hs, low),
        grid=(3 * groups,),
        out_shape=jax.ShapeDtypeStruct((tokens, heads * hd), BF),
        in_specs=[
            pl.BlockSpec(memory_space=pltpu.SMEM),
            pl.BlockSpec(wide, second),
            pl.BlockSpec(wide, both),
            pl.BlockSpec(wide, both),
            row_block,
            row_block,
            pl.BlockSpec(level_weights.shape, lambda i: (0, 0, 0)),
            pl.BlockSpec((1, hs * hd), third),
        ],
        out_specs=pl.BlockSpec(wide, third),
        scratch_shapes=[
            pltpu.VMEM((tokens, tokens), F32),
            pltpu.VMEM((heads, tokens), F32),
            pltpu.VMEM((groups, hs, 3, half, half), BF),
            pltpu.VMEM((groups, tokens, hs * hd), BF),
            pltpu.VMEM((groups, tokens, hs * hd), F32),
            pltpu.VMEM((groups, tokens, hs * hd), BF),
            pltpu.VMEM((nbits, groups, 2, hs, hd, hd), BF),
            pltpu.VMEM((nbits, groups, 2, hs, hd, hd), BF),
            pltpu.VMEM((groups, hs, hd, hd), F32),
            pltpu.VMEM((nbits, groups, hs, hd, hd), BF),
            pltpu.SemaphoreType.DMA((nbits, groups)),
            pltpu.SemaphoreType.DMA((nbits, groups)),
        ],
        compiler_params=pltpu.CompilerParams(
            collective_id=1, has_side_effects=True, vmem_limit_bytes=56 * 2**20
        ),
        name="mixer",
    )(doc_start, queries, keys, values, log_decay, beta, level_weights, norm_gain.reshape(1, -1))


def project_kernel(
    chunk, z_ref, w_hbm, out_ref, w_ref, keep, send_a, recv_a, send_y, recv_y, send_b, recv_b,
    w_sem, sa_sem, ra_sem, sy_sem, ry_sem, sb_sem, rb_sem,
):
    me = lax.axis_index("head")
    mate = me + 1 - 2 * (me % 2)
    across = (me + 2) % 4
    far_mate = (mate + 2) % 4
    count = keep.shape[1]
    rows = keep.shape[2]

    def columns(j):
        return pl.ds(pl.multiple_of(j * chunk, chunk), chunk)

    def load(j):
        return pltpu.make_async_copy(w_hbm.at[:, columns(j)], w_ref.at[:, columns(j)], w_sem.at[j])

    def remote(src, dst, ssem, rsem, j, target):
        return pltpu.make_async_remote_copy(
            src_ref=src.at[j],
            dst_ref=dst.at[j],
            send_sem=ssem.at[j],
            recv_sem=rsem.at[j],
            device_id={"head": target},
            device_id_type=pl.DeviceIdType.MESH,
        )

    def copy_a(j):
        return remote(send_a, recv_a, sa_sem, ra_sem, j, mate)

    def copy_b(j):
        return remote(send_b, recv_b, sb_sem, rb_sem, j, mate)

    def copy_y(j):
        return remote(send_y, recv_y, sy_sem, ry_sem, j, across)

    def block(owner):
        return z_ref[pl.ds(pl.multiple_of(owner * rows, rows), rows), :]

    lax.fori_loop(0, count, lambda j, _: (load(j).start(), 0)[1], 0)
    barrier = pltpu.get_barrier_semaphore()
    for other in (mate, across):
        pl.semaphore_signal(
            barrier, inc=1, device_id={"head": other}, device_id_type=pl.DeviceIdType.MESH
        )
    pl.semaphore_wait(barrier, 2)

    def forward(j):
        copy_a(j).wait_recv()
        send_y[j] = (keep[0, j] + recv_a[j].astype(F32)).astype(BF)
        copy_y(j).start()

    def far(j, _):
        load(j).wait()
        weight = w_ref[:, columns(j)]
        send_a[j] = jnp.dot(block(far_mate), weight, preferred_element_type=F32).astype(BF)
        copy_a(j).start()
        keep[0, j] = jnp.dot(block(across), weight, preferred_element_type=F32)

        @pl.when(j > 0)
        def _():
            forward(j - 1)

        return 0

    lax.fori_loop(0, count, far, 0)
    forward(count - 1)

    def near(j, _):
        weight = w_ref[:, columns(j)]
        send_b[j] = jnp.dot(block(mate), weight, preferred_element_type=F32).astype(BF)
        copy_b(j).start()
        keep[1, j] = jnp.dot(block(me), weight, preferred_element_type=F32)
        return 0

    lax.fori_loop(0, count, near, 0)

    def close(j, _):
        copy_b(j).wait_recv()
        copy_y(j).wait_recv()
        total = keep[1, j] + recv_b[j].astype(F32) + recv_y[j].astype(F32)
        out_ref[:, columns(j)] = total.astype(BF)
        copy_a(j).wait_send()
        copy_b(j).wait_send()
        copy_y(j).wait_send()
        return 0

    lax.fori_loop(0, count, close, 0)


def project(normed, out_weight):
    tokens, width = normed.shape
    out_width = out_weight.shape[1]
    rows = tokens // 4
    chunk = min(512, out_width)
    count = out_width // chunk
    slab = pltpu.VMEM((count, rows, chunk), BF)
    sems = [pltpu.SemaphoreType.DMA((count,))] * 7
    return pl.pallas_call(
        functools.partial(project_kernel, chunk),
        out_shape=jax.ShapeDtypeStruct((rows, out_width), BF),
        in_specs=[pl.BlockSpec(memory_space=pltpu.VMEM), pl.BlockSpec(memory_space=pl.ANY)],
        out_specs=pl.BlockSpec(memory_space=pltpu.VMEM),
        scratch_shapes=[
            pltpu.VMEM((width, out_width), BF),
            pltpu.VMEM((2, count, rows, chunk), F32),
        ]
        + [slab] * 6
        + sems,
        compiler_params=pltpu.CompilerParams(
            collective_id=0, has_side_effects=True, vmem_limit_bytes=56 * 2**20
        ),
        name="project",
    )(normed, out_weight)


def body(queries, keys, values, log_decay, beta, level_weights, doc_start, norm_gain, out_weight):
    normed = mixer(
        queries, keys, values, log_decay, beta, level_weights, doc_start, norm_gain
    )
    return project(normed, out_weight)


def solution(mesh):
    placed = (
        P("seq", "head"),
        P("seq", "head"),
        P("seq", "head"),
        P("head", "seq"),
        P("head", "seq"),
        P(None, "head", "seq"),
        P("seq"),
        P("head"),
        P("head", None),
    )
    return jax.shard_map(
        body, mesh=mesh, in_specs=placed, out_specs=P(("seq", "head"), None), check_vma=False
    )
```

```python
import functools

import jax
import jax.numpy as jnp
from jax import lax
from jax.experimental import pallas as pl
from jax.experimental.pallas import tpu as pltpu
from jax.sharding import PartitionSpec as P

SPAN = 64
EPS = 1e-06
BF = jnp.bfloat16
F32 = jnp.float32


def mm(a, b):
    return jnp.dot(a.astype(BF), b.astype(BF), preferred_element_type=F32)


def mm_nt(a, b):
    return lax.dot_general(
        a.astype(BF), b.astype(BF), (((1,), (1,)), ((), ())), preferred_element_type=F32
    )


def mm_tn(a, b):
    return lax.dot_general(
        a.astype(BF), b.astype(BF), (((0,), (0,)), ((), ())), preferred_element_type=F32
    )


def normalize(vector):
    return vector * lax.rsqrt(jnp.sum(vector * vector, axis=-1, keepdims=True) + EPS)


def prefix_sum(rows):
    lane = lax.broadcasted_iota(jnp.int32, rows.shape, 1)
    reach = 1
    while reach < rows.shape[1]:
        rows = rows + jnp.where(lane >= reach, pltpu.roll(rows, reach, 1), 0.0)
        reach *= 2
    return rows


def document_ids(doc_ref, shape, dim):
    span = lax.broadcasted_iota(jnp.int32, shape, dim) // SPAN
    ids = jnp.zeros(shape, jnp.int32)
    for c in range(doc_ref.shape[0]):
        ids = ids + jnp.where(span >= c, doc_ref[c], 0)
    return ids


def fill_bias(doc_ref, bias_ref):
    tokens = bias_ref.shape[0]
    ids_col = document_ids(doc_ref, (tokens, 1), 0)
    ids_row = document_ids(doc_ref, (1, tokens), 1)
    rows = lax.broadcasted_iota(jnp.int32, (tokens, tokens), 0)
    cols = lax.broadcasted_iota(jnp.int32, (tokens, tokens), 1)
    valid = (rows >= cols) & (ids_col == ids_row)
    bias_ref[...] = jnp.where(valid, 0.0, -1e30)


def columns_of(rows):
    count, tokens = rows[0].shape[0] * len(rows), rows[0].shape[1]
    pad = -count % 8
    if pad:
        rows = rows + [jnp.zeros((pad, tokens), F32)]
    return jnp.concatenate(rows, axis=0).T


def unit_lower_inverses(lowers):
    size = lowers[0].shape[0]
    rows = lax.broadcasted_iota(jnp.int32, (size, size), 0)
    cols = lax.broadcasted_iota(jnp.int32, (size, size), 1)
    apart = rows ^ cols
    eye = jnp.where(apart == 0, 1.0, 0.0)
    base = 16
    inside = (apart < base) & (apart > 0)
    powers = [jnp.where(inside, lower, 0.0) for lower in lowers]
    inverses = [eye - power for power in powers]
    powers = [mm(power, power) for power in powers]
    reach = 2
    while reach < base:
        if 2 * reach < base:
            both = [
                mm(jnp.concatenate([power.astype(BF), inverse.astype(BF)], axis=0), power)
                for power, inverse in zip(powers, inverses)
            ]
            powers = [pair[:size] for pair in both]
            inverses = [inverse + pair[size:] for inverse, pair in zip(inverses, both)]
        else:
            inverses = [inverse + mm(inverse, power) for power, inverse in zip(powers, inverses)]
        reach *= 2
    while base < size:
        band = (apart >= base) & (apart < 2 * base)
        offs = [jnp.where(band, lower, 0.0).astype(BF) for lower in lowers]
        held = [inverse.astype(BF) for inverse in inverses]
        steps = [mm(inverse, off) for inverse, off in zip(held, offs)]
        steps = [mm(first, inverse) for first, inverse in zip(steps, held)]
        inverses = [inverse - step for inverse, step in zip(inverses, steps)]
        base *= 2
    return [inverse.astype(BF) for inverse in inverses]


def form_maps(step, heads_step, doc_ref, k_ref, v_ref, beta_ref, inv_ref, erase_ref, map_ref, bias_ref, cum_ref):
    tokens = k_ref.shape[0]
    half = tokens // 2
    ids_col = document_ids(doc_ref, (tokens, 1), 0)
    first_doc = ids_col == 0
    last_doc = ids_col == jnp.max(ids_col)
    hd = 128
    eye = jnp.where(
        lax.broadcasted_iota(jnp.int32, (hd, hd), 0) == lax.broadcasted_iota(jnp.int32, (hd, hd), 1),
        1.0,
        0.0,
    )
    heads = range(heads_step)
    col_of = [slice(j * hd, (j + 1) * hd) for j in heads]
    keys = [normalize(k_ref[:, c].astype(F32)) for c in col_of]
    keys_b = [key.astype(BF) for key in keys]
    cum_rows = [cum_ref[pl.ds(step * heads_step + j, 1), :] for j in heads]
    sides = [
        columns_of([cum_rows[j], beta_ref[pl.ds(step * heads_step + j, 1), :]]) for j in heads
    ]
    cums, betas = [side[:, 0:1] for side in sides], [side[:, 1:2] for side in sides]
    quarter = half // 2
    parts = tokens // quarter

    def lower(j, rs, cs):
        ratio = jnp.exp(cums[j][rs] - cum_rows[j][:, cs] + bias_ref[rs, cs])
        return ratio * mm_nt(keys_b[j][rs], keys_b[j][cs]) * betas[j][rs]

    piece = [slice(i * quarter, (i + 1) * quarter) for i in range(parts)]
    diagonal = unit_lower_inverses([lower(j, p, p) for j in heads for p in piece])
    merges = [(j, i) for j in heads for i in range(0, parts, 2)]
    firsts = [
        mm(diagonal[j * parts + i + 1], lower(j, piece[i + 1], piece[i])) for j, i in merges
    ]
    corners = [
        -mm(first, diagonal[j * parts + i]) for first, (j, i) in zip(firsts, merges)
    ]
    inverses = []
    for corner, (j, i) in zip(corners, merges):
        a, b = diagonal[j * parts + i], diagonal[j * parts + i + 1]
        top = jnp.concatenate([a, jnp.zeros_like(a)], axis=1)
        inverses.append(
            jnp.concatenate([top, jnp.concatenate([corner.astype(BF), b], axis=1)], axis=0)
        )
    low, high = slice(0, half), slice(half, tokens)
    firsts = [mm(inverses[2 * j + 1], lower(j, high, low)) for j in heads]
    cross = [(-mm(first, inverses[2 * j])).astype(BF) for j, first in enumerate(firsts)]
    for j in heads:
        c, key, cum, beta = col_of[j], keys[j], cums[j], betas[j]
        inv0, inv10, inv1 = inverses[2 * j], cross[j], inverses[2 * j + 1]
        inv_ref[step, j, 0] = inv0
        inv_ref[step, j, 1] = inv10
        inv_ref[step, j, 2] = inv1
        gamma = jnp.where(first_doc, jnp.exp(cum), 0.0)
        tail = jnp.where(last_doc, jnp.exp(cum_rows[j][:, tokens - 1 : tokens] - cum), 0.0)
        rhs = jnp.concatenate(
            [beta * v_ref[:, c].astype(F32), (beta * gamma) * key], axis=1
        ).astype(BF)
        solved0 = mm(inv0, rhs[:half])
        solved1 = mm(inv10, rhs[:half]) + mm(inv1, rhs[half:])
        solved = jnp.concatenate([solved0, solved1], axis=0).astype(BF)
        erase_ref[step, :, c] = solved[:, hd:]
        out = mm_tn(tail * key, solved)
        map_ref[0, step, 0, j] = (gamma[tokens - 1 : tokens, :] * eye - out[:, hd:]).astype(BF)
        map_ref[0, step, 1, j] = out[:, :hd].astype(BF)


def read_block(step, heads_step, doc_ref, q_ref, k_ref, v_ref, beta_ref, w_ref, inv_ref, erase_ref, y_ref, reader_ref, bias_ref, cum_ref):
    tokens = k_ref.shape[0]
    half = tokens // 2
    quarter = half // 2
    first = document_ids(doc_ref, (tokens, 1), 0) == 0
    hd = 128
    rows = lax.broadcasted_iota(jnp.int32, (quarter, quarter), 0)
    cols_i = lax.broadcasted_iota(jnp.int32, (quarter, quarter), 1)
    same_span = (rows ^ cols_i) < SPAN
    for j in range(heads_step):
        h = step * heads_step + j
        cols = slice(j * hd, (j + 1) * hd)
        key_b = normalize(k_ref[:, cols].astype(F32)).astype(BF)
        query = normalize(q_ref[:, cols].astype(F32))
        query_b = query.astype(BF)
        cum_row = cum_ref[pl.ds(h, 1), :]
        side = columns_of(
            [cum_row, beta_ref[pl.ds(h, 1), :]] + [w_ref[l, pl.ds(h, 1), :] for l in range(4)]
        )
        cum, beta = side[:, 0:1], side[:, 1:2]
        weights = [side[:, 2 + l : 3 + l] for l in range(4)]
        gamma = jnp.where(first, jnp.exp(cum), 0.0)

        def scores(r, c):
            rs, cs = slice(r * half, (r + 1) * half), slice(c * half, (c + 1) * half)
            ratio = jnp.exp(cum[rs] - cum_row[:, cs] + bias_ref[rs, cs])
            return (ratio * mm_nt(query_b[rs], key_b[cs])).astype(BF)

        def within(block, r):
            lo = r * half
            mid = lo + quarter
            a = block[:quarter, :quarter]
            a = a * jnp.where(same_span, weights[0][lo:mid], weights[1][lo:mid])
            b = block[quarter:, :quarter] * weights[2][mid : mid + quarter]
            c = block[quarter:, quarter:]
            c = c * jnp.where(
                same_span, weights[0][mid : mid + quarter], weights[1][mid : mid + quarter]
            )
            top = jnp.concatenate([a, jnp.zeros_like(a)], axis=1)
            return jnp.concatenate([top, jnp.concatenate([b, c], axis=1)], axis=0)

        s00, s10, s11 = scores(0, 0), scores(1, 0), scores(1, 1)
        inv0, inv10, inv1 = inv_ref[step, j, 0], inv_ref[step, j, 1], inv_ref[step, j, 2]
        r00 = within(mm(s00, inv0), 0)
        r11 = within(mm(s11, inv1), 1)
        r10 = (mm(s10, inv0) + mm(s11, inv10)) * weights[3][half:]
        value = (beta * v_ref[:, cols].astype(F32)).astype(BF)
        y_ref[step, :half, cols] = mm(r00, value[:half])
        y_ref[step, half:, cols] = mm(r10, value[:half]) + mm(r11, value[half:])
        erase = erase_ref[step, :, cols]
        reader_ref[step, :half, cols] = (gamma[:half] * query[:half] - mm(s00, erase[:half])).astype(BF)
        reader_ref[step, half:, cols] = (
            gamma[half:] * query[half:] - mm(s10, erase[:half]) - mm(s11, erase[half:])
        ).astype(BF)


def finish_rows(half_idx, hs, low, y_ref, reader_ref, state_ref, w_ref, gain_ref, z_ref):
    hd = 128
    levels = state_ref.shape[0]
    half = z_ref.shape[0] // 2
    part = pl.ds(pl.multiple_of(half_idx * half, half), half)

    def group(g, _):
        for j in range(hs):
            h = g * hs + j
            cols = slice(j * hd, (j + 1) * hd)
            out_cols = pl.ds(pl.multiple_of(h * hd, hd), hd)
            side = columns_of([w_ref[low + l, pl.ds(h, 1), part] for l in range(levels)])
            y = y_ref[g, part, cols]
            reader = reader_ref[g, part, cols]
            for l in range(levels):
                y = y + side[:, l : l + 1] * mm(reader, state_ref[l, g, j])
            y = y * lax.rsqrt(jnp.mean(y * y, axis=-1, keepdims=True) + EPS)
            z_ref[part, out_cols] = (y * gain_ref[:, out_cols]).astype(BF)
        return 0

    lax.fori_loop(0, state_ref.shape[1], group, 0)


def project_rows(me, finish, weight_load, z_ref, w_ref, out_ref, keep, slabs, sems):
    mate = me + 1 - 2 * (me % 2)
    across = (me + 2) % 4
    send_a, recv_a, send_y, recv_y, send_b, recv_b = slabs
    sa_sem, ra_sem, sy_sem, ry_sem, sb_sem, rb_sem = sems
    count, rows, chunk = keep.shape[1:]
    near = me // 2
    far = 1 - near

    def columns(j):
        return pl.ds(pl.multiple_of(j * chunk, chunk), chunk)

    def remote(src, dst, ssem, rsem, j, target):
        return pltpu.make_async_remote_copy(
            src_ref=src.at[j],
            dst_ref=dst.at[j],
            send_sem=ssem.at[j],
            recv_sem=rsem.at[j],
            device_id={"head": target},
            device_id_type=pl.DeviceIdType.MESH,
        )

    def copy_a(j):
        return remote(send_a, recv_a, sa_sem, ra_sem, j, mate)

    def copy_b(j):
        return remote(send_b, recv_b, sb_sem, rb_sem, j, mate)

    def copy_y(j):
        return remote(send_y, recv_y, sy_sem, ry_sem, j, across)

    def terms(half_idx, j):
        part = pl.ds(pl.multiple_of(half_idx * 2 * rows, 2 * rows), 2 * rows)
        product = jnp.dot(z_ref[part, :], w_ref[:, columns(j)], preferred_element_type=F32)
        first = me % 2 == 0
        top, bottom = product[:rows], product[rows:]
        return jnp.where(first, top, bottom), jnp.where(first, bottom, top)

    def forward(j):
        copy_a(j).wait_recv()
        send_y[j] = (keep[0, j] + recv_a[j].astype(F32)).astype(BF)
        copy_y(j).start()

    def far_step(j, _):
        weight_load(j).wait()
        mine, other = terms(far, j)
        send_a[j] = other.astype(BF)
        copy_a(j).start()
        keep[0, j] = mine

        @pl.when(j > 0)
        def _():
            forward(j - 1)

        return 0

    def near_step(j, _):
        mine, other = terms(near, j)
        send_b[j] = other.astype(BF)
        copy_b(j).start()
        keep[1, j] = mine
        return 0

    def close(j, _):
        copy_b(j).wait_recv()
        copy_y(j).wait_recv()
        total = keep[1, j] + recv_b[j].astype(F32) + recv_y[j].astype(F32)
        out_ref[:, columns(j)] = total.astype(BF)
        copy_a(j).wait_send()
        copy_b(j).wait_send()
        copy_y(j).wait_send()
        return 0

    finish(far)
    lax.fori_loop(0, count, far_step, 0)
    forward(count - 1)
    finish(near)
    lax.fori_loop(0, count, near_step, 0)
    lax.fori_loop(0, count, close, 0)


def layer_kernel(
    hs, low, doc_ref, q_ref, k_ref, v_ref, log_ref, beta_ref, w_ref, gain_ref, weight_hbm, out_ref,
    bias_ref, cum_ref, inv_ref, erase_ref, y_ref, reader_ref, send, recv, carried, states,
    z_ref, weight_ref, keep, send_a, recv_a, send_y, recv_y, send_b, recv_b,
    send_sem, recv_sem, load_sem, sa_sem, ra_sem, sy_sem, ry_sem, sb_sem, rb_sem,
):
    step = pl.program_id(0)
    nbits, groups = send.shape[0], send.shape[1]
    hd = send.shape[-1]
    block = lax.axis_index("seq")
    me = lax.axis_index("head")
    mate = me + 1 - 2 * (me % 2)
    across = (me + 2) % 4
    count, chunk = keep.shape[1], keep.shape[3]
    barrier = pltpu.get_barrier_semaphore()

    def partner(bit):
        return block + (1 << bit) * (1 - 2 * ((block // (1 << bit)) % 2))

    def copy(bit, g):
        whole = bit < nbits - 1
        return pltpu.make_async_remote_copy(
            src_ref=send.at[bit, g] if whole else send.at[bit, g, 1],
            dst_ref=recv.at[bit, g] if whole else recv.at[bit, g, 1],
            send_sem=send_sem.at[bit, g],
            recv_sem=recv_sem.at[bit, g],
            device_id={"seq": partner(bit)},
            device_id_type=pl.DeviceIdType.MESH,
        )

    def weight_load(j):
        cols = pl.ds(pl.multiple_of(j * chunk, chunk), chunk)
        return pltpu.make_async_copy(weight_hbm.at[:, cols], weight_ref.at[:, cols], load_sem.at[j])

    @pl.when(step == 0)
    def _():
        for other in (mate, across):
            pl.semaphore_signal(
                barrier, inc=1, device_id={"head": other}, device_id_type=pl.DeviceIdType.MESH
            )
        for bit in range(nbits):
            pl.semaphore_signal(
                barrier, inc=1, device_id={"seq": partner(bit)}, device_id_type=pl.DeviceIdType.MESH
            )
        fill_bias(doc_ref, bias_ref)
        cum_ref[...] = prefix_sum(log_ref[...])
        lax.fori_loop(0, count, lambda j, _: (weight_load(j).start(), 0)[1], 0)

    @pl.when(step < groups)
    def _():
        form_maps(
            step, hs, doc_ref, k_ref, v_ref, beta_ref, inv_ref, erase_ref, send, bias_ref, cum_ref
        )

    @pl.when(step == 0)
    def _():
        pl.semaphore_wait(barrier, nbits + 2)

    @pl.when(step < groups)
    def _():
        copy(0, step).start()

    @pl.when((step >= groups) & (step < 2 * groups))
    def _():
        read_block(
            step - groups, hs, doc_ref, q_ref, k_ref, v_ref, beta_ref, w_ref, inv_ref, erase_ref,
            y_ref, reader_ref, bias_ref, cum_ref,
        )

    def exchange(bit, g):
        copy(bit, g).wait_recv()
        upper = (block // (1 << bit)) % 2 == 1
        eye = jnp.where(
            lax.broadcasted_iota(jnp.int32, (hd, hd), 0)
            == lax.broadcasted_iota(jnp.int32, (hd, hd), 1),
            1.0,
            0.0,
        )
        more = bit < nbits - 1
        for j in range(hs):
            sib_s = recv[bit, g, 1, j]
            if more:
                sib_t = recv[bit, g, 0, j]
            if bit == 0:
                reached_s = sib_s.astype(F32)
                if more:
                    carried[g, j] = jnp.where(upper, sib_t.astype(F32), eye)
            elif more:
                held = carried[g, j]
                both = mm(held, jnp.concatenate([sib_t, sib_s], axis=1))
                reached_s = both[:, hd:]
                carried[g, j] = jnp.where(upper, both[:, :hd], held)
            else:
                reached_s = mm(carried[g, j], sib_s)
            states[bit, g, j] = jnp.where(upper, reached_s, 0.0).astype(BF)
            if more:
                sib = jnp.concatenate([sib_t, sib_s], axis=1).astype(F32)
                own = jnp.concatenate([send[bit, g, 0, j], send[bit, g, 1, j]], axis=1).astype(F32)
                first = jnp.where(upper, sib, own)
                second = jnp.where(upper, own, sib)
                merged = mm(second[:, :hd], first)
                send[bit + 1, g, 0, j] = merged[:, :hd].astype(BF)
                send[bit + 1, g, 1, j] = (merged[:, hd:] + second[:, hd:]).astype(BF)
        if more:
            copy(bit + 1, g).start()

    for bit in range(nbits):
        g = step - 1 - bit

        @pl.when((step < 2 * groups) & (g >= 0) & (g < groups))
        def _(bit=bit, g=g):
            exchange(bit, g)

    @pl.when(step == 2 * groups)
    def _():
        for late in range(2 * groups, groups + nbits):
            for bit in range(nbits):
                if 0 <= late - 1 - bit < groups:
                    exchange(bit, late - 1 - bit)

        def finish(half_idx):
            finish_rows(half_idx, hs, low, y_ref, reader_ref, states, w_ref, gain_ref, z_ref)

        project_rows(
            me,
            finish,
            weight_load,
            z_ref,
            weight_ref,
            out_ref,
            keep,
            (send_a, recv_a, send_y, recv_y, send_b, recv_b),
            (sa_sem, ra_sem, sy_sem, ry_sem, sb_sem, rb_sem),
        )
        for bit in range(nbits):
            for g in range(groups):
                copy(bit, g).wait_send()


def body(queries, keys, values, log_decay, beta, level_weights, doc_start, norm_gain, out_weight):
    tokens = queries.shape[0]
    heads = log_decay.shape[0]
    hd = queries.shape[1] // heads
    half = tokens // 2
    hs = 2
    groups = heads // hs
    low = (tokens // SPAN).bit_length()
    nbits = lax.axis_size("seq").bit_length() - 1
    wide = (tokens, hs * hd)
    rows = tokens // lax.axis_size("head")
    out_width = out_weight.shape[1]
    chunk = min(512, out_width)
    count = out_width // chunk

    def both(i):
        return (0, jnp.minimum(i, 2 * groups - 1) % groups)

    def second(i):
        return (0, jnp.clip(i - groups, 0, groups - 1))

    row_block = pl.BlockSpec((heads, tokens), lambda i: (0, 0))
    return pl.pallas_call(
        functools.partial(layer_kernel, hs, low),
        grid=(2 * groups + 1,),
        out_shape=jax.ShapeDtypeStruct((rows, out_width), BF),
        in_specs=[
            pl.BlockSpec(memory_space=pltpu.SMEM),
            pl.BlockSpec(wide, second),
            pl.BlockSpec(wide, both),
            pl.BlockSpec(wide, both),
            row_block,
            row_block,
            pl.BlockSpec(level_weights.shape, lambda i: (0, 0, 0)),
            pl.BlockSpec((1, heads * hd), lambda i: (0, 0)),
            pl.BlockSpec(memory_space=pl.ANY),
        ],
        out_specs=pl.BlockSpec((rows, out_width), lambda i: (0, 0)),
        scratch_shapes=[
            pltpu.VMEM((tokens, tokens), F32),
            pltpu.VMEM((heads, tokens), F32),
            pltpu.VMEM((groups, hs, 3, half, half), BF),
            pltpu.VMEM((groups, tokens, hs * hd), BF),
            pltpu.VMEM((groups, tokens, hs * hd), F32),
            pltpu.VMEM((groups, tokens, hs * hd), BF),
            pltpu.VMEM((nbits, groups, 2, hs, hd, hd), BF),
            pltpu.VMEM((nbits, groups, 2, hs, hd, hd), BF),
            pltpu.VMEM((groups, hs, hd, hd), F32),
            pltpu.VMEM((nbits, groups, hs, hd, hd), BF),
            pltpu.VMEM((tokens, heads * hd), BF),
            pltpu.VMEM(out_weight.shape, BF),
            pltpu.VMEM((2, count, rows, chunk), F32),
        ]
        + [pltpu.VMEM((count, rows, chunk), BF)] * 6
        + [pltpu.SemaphoreType.DMA((nbits, groups))] * 2
        + [pltpu.SemaphoreType.DMA((count,))] * 7,
        compiler_params=pltpu.CompilerParams(
            collective_id=0, has_side_effects=True, vmem_limit_bytes=56 * 2**20
        ),
        name="layer",
    )(
        doc_start, queries, keys, values, log_decay, beta, level_weights,
        norm_gain.reshape(1, -1), out_weight,
    )


def solution(mesh):
    placed = (
        P("seq", "head"),
        P("seq", "head"),
        P("seq", "head"),
        P("head", "seq"),
        P("head", "seq"),
        P(None, "head", "seq"),
        P("seq"),
        P("head"),
        P("head", None),
    )
    return jax.shard_map(
        body, mesh=mesh, in_specs=placed, out_specs=P(("seq", "head"), None), check_vma=False
    )
```

```python
import functools

import jax
import jax.numpy as jnp
from jax import lax
from jax.experimental import pallas as pl
from jax.experimental.pallas import tpu as pltpu
from jax.sharding import PartitionSpec as P

SPAN = 64
EPS = 1e-06
BF = jnp.bfloat16
F32 = jnp.float32


def mm(a, b):
    return jnp.dot(a.astype(BF), b.astype(BF), preferred_element_type=F32)


def mm_nt(a, b):
    return lax.dot_general(
        a.astype(BF), b.astype(BF), (((1,), (1,)), ((), ())), preferred_element_type=F32
    )


def mm_tn(a, b):
    return lax.dot_general(
        a.astype(BF), b.astype(BF), (((0,), (0,)), ((), ())), preferred_element_type=F32
    )


def normalize(vector):
    return vector * lax.rsqrt(jnp.sum(vector * vector, axis=-1, keepdims=True) + EPS)


def prefix_sum(rows):
    lane = lax.broadcasted_iota(jnp.int32, rows.shape, 1)
    reach = 1
    while reach < rows.shape[1]:
        rows = rows + jnp.where(lane >= reach, pltpu.roll(rows, reach, 1), 0.0)
        reach *= 2
    return rows


def document_ids(doc_ref, shape, dim):
    span = lax.broadcasted_iota(jnp.int32, shape, dim) // SPAN
    ids = jnp.zeros(shape, jnp.int32)
    for c in range(doc_ref.shape[0]):
        ids = ids + jnp.where(span >= c, doc_ref[c], 0)
    return ids


def fill_bias(doc_ref, bias_ref):
    tokens = bias_ref.shape[0]
    ids_col = document_ids(doc_ref, (tokens, 1), 0)
    ids_row = document_ids(doc_ref, (1, tokens), 1)
    rows = lax.broadcasted_iota(jnp.int32, (tokens, tokens), 0)
    cols = lax.broadcasted_iota(jnp.int32, (tokens, tokens), 1)
    valid = (rows >= cols) & (ids_col == ids_row)
    bias_ref[...] = jnp.where(valid, 0.0, -1e30)


def columns_of(rows):
    count, tokens = rows[0].shape[0] * len(rows), rows[0].shape[1]
    pad = -count % 8
    if pad:
        rows = rows + [jnp.zeros((pad, tokens), F32)]
    return jnp.concatenate(rows, axis=0).T


def pair_diagonal(pair):
    size = pair.shape[0]
    pair = pair.astype(BF)
    zero = jnp.zeros((size, size), BF)
    top = jnp.concatenate([pair[:, :size], zero], axis=1)
    return jnp.concatenate([top, jnp.concatenate([zero, pair[:, size:]], axis=1)], axis=0)


def unit_lower_inverses(pairs):
    size = pairs[0].shape[0]
    rows = lax.broadcasted_iota(jnp.int32, (size, 2 * size), 0)
    cols = lax.broadcasted_iota(jnp.int32, (size, 2 * size), 1)
    apart = rows ^ (cols % size)
    eye = jnp.where(apart == 0, 1.0, 0.0)
    base = 16
    inside = (apart < base) & (apart > 0)
    powers = [jnp.where(inside, pair, 0.0) for pair in pairs]
    inverses = [eye - power for power in powers]
    powers = [mm(power, pair_diagonal(power)) for power in powers]
    reach = 2
    while reach < base:
        if 2 * reach < base:
            both = [
                mm(
                    jnp.concatenate([power.astype(BF), inverse.astype(BF)], axis=0),
                    pair_diagonal(power),
                )
                for power, inverse in zip(powers, inverses)
            ]
            powers = [item[:size] for item in both]
            inverses = [inverse + item[size:] for inverse, item in zip(inverses, both)]
        else:
            inverses = [
                inverse + mm(inverse, pair_diagonal(power))
                for power, inverse in zip(powers, inverses)
            ]
        reach *= 2
    while base < size:
        band = (apart >= base) & (apart < 2 * base)
        offs = [pair_diagonal(jnp.where(band, pair, 0.0)) for pair in pairs]
        held = [inverse.astype(BF) for inverse in inverses]
        steps = [mm(inverse, off) for inverse, off in zip(held, offs)]
        steps = [mm(first, pair_diagonal(inverse)) for first, inverse in zip(steps, held)]
        inverses = [inverse - step for inverse, step in zip(inverses, steps)]
        base *= 2
    return [inverse.astype(BF) for inverse in inverses]


def form_maps(step, heads_step, doc_ref, k_ref, v_ref, beta_ref, inv_ref, erase_ref, map_ref, bias_ref, cum_ref):
    tokens = k_ref.shape[0]
    half = tokens // 2
    ids_col = document_ids(doc_ref, (tokens, 1), 0)
    first_doc = ids_col == 0
    last_doc = ids_col == jnp.max(ids_col)
    hd = 128
    eye = jnp.where(
        lax.broadcasted_iota(jnp.int32, (hd, hd), 0) == lax.broadcasted_iota(jnp.int32, (hd, hd), 1),
        1.0,
        0.0,
    )
    heads = range(heads_step)
    col_of = [slice(j * hd, (j + 1) * hd) for j in heads]
    keys = [normalize(k_ref[:, c].astype(F32)) for c in col_of]
    keys_b = [key.astype(BF) for key in keys]
    cum_rows = [cum_ref[pl.ds(step * heads_step + j, 1), :] for j in heads]
    sides = [
        columns_of([cum_rows[j], beta_ref[pl.ds(step * heads_step + j, 1), :]]) for j in heads
    ]
    cums, betas = [side[:, 0:1] for side in sides], [side[:, 1:2] for side in sides]
    quarter = half // 2
    parts = tokens // quarter

    def lower(j, rs, cs):
        ratio = jnp.exp(cums[j][rs] - cum_rows[j][:, cs] + bias_ref[rs, cs])
        return ratio * mm_nt(keys_b[j][rs], keys_b[j][cs]) * betas[j][rs]

    piece = [slice(i * quarter, (i + 1) * quarter) for i in range(parts)]
    merges = [(j, i) for j in heads for i in range(0, parts, 2)]
    paired = unit_lower_inverses(
        [
            jnp.concatenate([lower(j, piece[i + k], piece[i + k]) for k in range(2)], axis=1)
            for j, i in merges
        ]
    )
    diagonal = [pair[:, k * quarter : (k + 1) * quarter] for pair in paired for k in range(2)]
    firsts = [
        mm(diagonal[j * parts + i + 1], lower(j, piece[i + 1], piece[i])) for j, i in merges
    ]
    corners = [
        -mm(first, diagonal[j * parts + i]) for first, (j, i) in zip(firsts, merges)
    ]
    inverses = []
    for corner, (j, i) in zip(corners, merges):
        a, b = diagonal[j * parts + i], diagonal[j * parts + i + 1]
        top = jnp.concatenate([a, jnp.zeros_like(a)], axis=1)
        inverses.append(
            jnp.concatenate([top, jnp.concatenate([corner.astype(BF), b], axis=1)], axis=0)
        )
    low, high = slice(0, half), slice(half, tokens)
    firsts = [mm(inverses[2 * j + 1], lower(j, high, low)) for j in heads]
    cross = [(-mm(first, inverses[2 * j])).astype(BF) for j, first in enumerate(firsts)]
    for j in heads:
        c, key, cum, beta = col_of[j], keys[j], cums[j], betas[j]
        inv0, inv10, inv1 = inverses[2 * j], cross[j], inverses[2 * j + 1]
        inv_ref[step, j, 0] = inv0
        inv_ref[step, j, 1] = inv10
        inv_ref[step, j, 2] = inv1
        gamma = jnp.where(first_doc, jnp.exp(cum), 0.0)
        tail = jnp.where(last_doc, jnp.exp(cum_rows[j][:, tokens - 1 : tokens] - cum), 0.0)
        rhs = jnp.concatenate(
            [beta * v_ref[:, c].astype(F32), (beta * gamma) * key], axis=1
        ).astype(BF)
        solved0 = mm(inv0, rhs[:half])
        solved1 = mm(inv10, rhs[:half]) + mm(inv1, rhs[half:])
        solved = jnp.concatenate([solved0, solved1], axis=0).astype(BF)
        erase_ref[step, :, c] = solved[:, hd:]
        out = mm_tn(tail * key, solved)
        map_ref[0, step, 0, j] = (gamma[tokens - 1 : tokens, :] * eye - out[:, hd:]).astype(BF)
        map_ref[0, step, 1, j] = out[:, :hd].astype(BF)


def read_half(which, step, heads_step, doc_ref, q_ref, k_ref, v_ref, beta_ref, w_ref, inv_ref, erase_ref, y_ref, reader_ref, bias_ref, cum_ref):
    tokens = k_ref.shape[0]
    half = tokens // 2
    quarter = half // 2
    first = document_ids(doc_ref, (tokens, 1), 0) == 0
    hd = 128
    rows = lax.broadcasted_iota(jnp.int32, (quarter, quarter), 0)
    cols_i = lax.broadcasted_iota(jnp.int32, (quarter, quarter), 1)
    same_span = (rows ^ cols_i) < SPAN
    for j in range(heads_step):
        h = step * heads_step + j
        cols = slice(j * hd, (j + 1) * hd)
        key_b = normalize(k_ref[:, cols].astype(F32)).astype(BF)
        query = normalize(q_ref[:, cols].astype(F32))
        query_b = query.astype(BF)
        cum_row = cum_ref[pl.ds(h, 1), :]
        side = columns_of(
            [cum_row, beta_ref[pl.ds(h, 1), :]] + [w_ref[l, pl.ds(h, 1), :] for l in range(4)]
        )
        cum, beta = side[:, 0:1], side[:, 1:2]
        weights = [side[:, 2 + l : 3 + l] for l in range(4)]
        gamma = jnp.where(first, jnp.exp(cum), 0.0)

        def scores(r, c):
            rs, cs = slice(r * half, (r + 1) * half), slice(c * half, (c + 1) * half)
            ratio = jnp.exp(cum[rs] - cum_row[:, cs] + bias_ref[rs, cs])
            return (ratio * mm_nt(query_b[rs], key_b[cs])).astype(BF)

        def within(block, r):
            lo = r * half
            mid = lo + quarter
            a = block[:quarter, :quarter]
            a = a * jnp.where(same_span, weights[0][lo:mid], weights[1][lo:mid])
            b = block[quarter:, :quarter] * weights[2][mid : mid + quarter]
            c = block[quarter:, quarter:]
            c = c * jnp.where(
                same_span, weights[0][mid : mid + quarter], weights[1][mid : mid + quarter]
            )
            top = jnp.concatenate([a, jnp.zeros_like(a)], axis=1)
            return jnp.concatenate([top, jnp.concatenate([b, c], axis=1)], axis=0)

        inv0, inv10, inv1 = inv_ref[step, j, 0], inv_ref[step, j, 1], inv_ref[step, j, 2]
        value = (beta * v_ref[:, cols].astype(F32)).astype(BF)
        erase = erase_ref[step, :, cols]
        if which == 0:
            s00 = scores(0, 0)
            r00 = within(mm(s00, inv0), 0)
            y_ref[step, :half, cols] = mm(r00, value[:half])
            reader_ref[step, :half, cols] = (
                gamma[:half] * query[:half] - mm(s00, erase[:half])
            ).astype(BF)
            continue
        s10, s11 = scores(1, 0), scores(1, 1)
        r11 = within(mm(s11, inv1), 1)
        r10 = (mm(s10, inv0) + mm(s11, inv10)) * weights[3][half:]
        y_ref[step, half:, cols] = mm(r10, value[:half]) + mm(r11, value[half:])
        reader_ref[step, half:, cols] = (
            gamma[half:] * query[half:] - mm(s10, erase[:half]) - mm(s11, erase[half:])
        ).astype(BF)


def finish_rows(half_idx, g, hs, low, y_ref, reader_ref, state_ref, w_ref, gain_ref, z_ref):
    hd = 128
    levels = state_ref.shape[0]
    half = z_ref.shape[0] // 2
    part = pl.ds(pl.multiple_of(half_idx * half, half), half)

    for j in range(hs):
        h = g * hs + j
        cols = slice(j * hd, (j + 1) * hd)
        out_cols = pl.ds(pl.multiple_of(h * hd, hd), hd)
        side = columns_of([w_ref[low + l, pl.ds(h, 1), part] for l in range(levels)])
        y = y_ref[g, part, cols]
        reader = reader_ref[g, part, cols]
        for l in range(levels):
            y = y + side[:, l : l + 1] * mm(reader, state_ref[l, g, j])
        y = y * lax.rsqrt(jnp.mean(y * y, axis=-1, keepdims=True) + EPS)
        z_ref[part, out_cols] = (y * gain_ref[:, out_cols]).astype(BF)


def project_rows(me, finish_far, finish_near, weight_load, z_ref, w_ref, out_ref, keep, slabs, sems):
    mate = me + 1 - 2 * (me % 2)
    across = (me + 2) % 4
    send_a, recv_a, send_y, recv_y, send_b, recv_b = slabs
    sa_sem, ra_sem, sy_sem, ry_sem, sb_sem, rb_sem = sems
    count, rows, chunk = keep.shape[1:]
    near = me // 2
    far = 1 - near

    def columns(j):
        return pl.ds(pl.multiple_of(j * chunk, chunk), chunk)

    def remote(src, dst, ssem, rsem, j, target):
        return pltpu.make_async_remote_copy(
            src_ref=src.at[j],
            dst_ref=dst.at[j],
            send_sem=ssem.at[j],
            recv_sem=rsem.at[j],
            device_id={"head": target},
            device_id_type=pl.DeviceIdType.MESH,
        )

    def copy_a(j):
        return remote(send_a, recv_a, sa_sem, ra_sem, j, mate)

    def copy_b(j):
        return remote(send_b, recv_b, sb_sem, rb_sem, j, mate)

    def copy_y(j):
        return remote(send_y, recv_y, sy_sem, ry_sem, j, across)

    def terms(half_idx, j):
        part = pl.ds(pl.multiple_of(half_idx * 2 * rows, 2 * rows), 2 * rows)
        product = jnp.dot(z_ref[part, :], w_ref[:, columns(j)], preferred_element_type=F32)
        first = me % 2 == 0
        top, bottom = product[:rows], product[rows:]
        return jnp.where(first, top, bottom), jnp.where(first, bottom, top)

    def forward(j):
        copy_a(j).wait_recv()
        send_y[j] = (keep[0, j] + recv_a[j].astype(F32)).astype(BF)
        copy_y(j).start()

    def far_step(j, _):
        weight_load(j).wait()
        mine, other = terms(far, j)
        send_a[j] = other.astype(BF)
        copy_a(j).start()
        keep[0, j] = mine

        @pl.when(j > 0)
        def _():
            forward(j - 1)

        return 0

    def near_step(j, _):
        mine, other = terms(near, j)
        send_b[j] = other.astype(BF)
        copy_b(j).start()
        keep[1, j] = mine
        return 0

    def close(j, _):
        copy_b(j).wait_recv()
        copy_y(j).wait_recv()
        total = keep[1, j] + recv_b[j].astype(F32) + recv_y[j].astype(F32)
        out_ref[:, columns(j)] = total.astype(BF)
        copy_a(j).wait_send()
        copy_b(j).wait_send()
        copy_y(j).wait_send()
        return 0

    finish_far(far)
    lax.fori_loop(0, count, far_step, 0)
    forward(count - 1)
    finish_near(near)
    lax.fori_loop(0, count, near_step, 0)
    lax.fori_loop(0, count, close, 0)


def exchange_slots(nbits, groups):
    form, first, second, hop = 4.6, 0.9, 1.7, 3.5
    times = [(form * (at + 1), (at, 1)) for at in range(groups)]
    now = form * groups
    for at in range(groups, 2 * groups):
        times += [(now + first, (at, 0)), (now + first + second, (at, 1))]
        now += first + second
    slots, late = {}, []
    for g in range(groups):
        sent = form * (g + 1)
        for bit in range(nbits):
            open_slots = [(t, key) for t, key in times if sent is not None and t >= sent + hop]
            if open_slots:
                sent, key = open_slots[0]
                slots.setdefault(key, []).append((bit, g))
            else:
                sent = None
                late.append((bit, g))
    return slots, late


def layer_kernel(
    hs, low, doc_ref, q_ref, k_ref, v_ref, log_ref, beta_ref, w_ref, gain_ref, weight_hbm, out_ref,
    bias_ref, cum_ref, inv_ref, erase_ref, y_ref, reader_ref, send, recv, carried, states,
    z_ref, weight_ref, keep, send_a, recv_a, send_y, recv_y, send_b, recv_b,
    send_sem, recv_sem, load_sem, sa_sem, ra_sem, sy_sem, ry_sem, sb_sem, rb_sem,
):
    step = pl.program_id(0)
    nbits, groups = send.shape[0], send.shape[1]
    hd = send.shape[-1]
    block = lax.axis_index("seq")
    me = lax.axis_index("head")
    mate = me + 1 - 2 * (me % 2)
    across = (me + 2) % 4
    count, chunk = keep.shape[1], keep.shape[3]
    barrier = pltpu.get_barrier_semaphore()

    def partner(bit):
        return block + (1 << bit) * (1 - 2 * ((block // (1 << bit)) % 2))

    def copy(bit, g):
        whole = bit < nbits - 1
        return pltpu.make_async_remote_copy(
            src_ref=send.at[bit, g] if whole else send.at[bit, g, 1],
            dst_ref=recv.at[bit, g] if whole else recv.at[bit, g, 1],
            send_sem=send_sem.at[bit, g],
            recv_sem=recv_sem.at[bit, g],
            device_id={"seq": partner(bit)},
            device_id_type=pl.DeviceIdType.MESH,
        )

    def weight_load(j):
        cols = pl.ds(pl.multiple_of(j * chunk, chunk), chunk)
        return pltpu.make_async_copy(weight_hbm.at[:, cols], weight_ref.at[:, cols], load_sem.at[j])

    @pl.when(step == 0)
    def _():
        for other in (mate, across):
            pl.semaphore_signal(
                barrier, inc=1, device_id={"head": other}, device_id_type=pl.DeviceIdType.MESH
            )
        for bit in range(nbits):
            pl.semaphore_signal(
                barrier, inc=1, device_id={"seq": partner(bit)}, device_id_type=pl.DeviceIdType.MESH
            )
        fill_bias(doc_ref, bias_ref)
        cum_ref[...] = prefix_sum(log_ref[...])
        lax.fori_loop(0, count, lambda j, _: (weight_load(j).start(), 0)[1], 0)

    @pl.when(step < groups)
    def _():
        form_maps(
            step, hs, doc_ref, k_ref, v_ref, beta_ref, inv_ref, erase_ref, send, bias_ref, cum_ref
        )

    @pl.when(step == 0)
    def _():
        pl.semaphore_wait(barrier, nbits + 2)

    def exchange(bit, g):
        copy(bit, g).wait_recv()
        upper = (block // (1 << bit)) % 2 == 1
        eye = jnp.where(
            lax.broadcasted_iota(jnp.int32, (hd, hd), 0)
            == lax.broadcasted_iota(jnp.int32, (hd, hd), 1),
            1.0,
            0.0,
        )
        more = bit < nbits - 1
        for j in range(hs):
            sib_s = recv[bit, g, 1, j]
            if more:
                sib_t = recv[bit, g, 0, j]
            if bit == 0:
                reached_s = sib_s.astype(F32)
                if more:
                    carried[g, j] = jnp.where(upper, sib_t.astype(F32), eye)
            elif more:
                held = carried[g, j]
                both = mm(held, jnp.concatenate([sib_t, sib_s], axis=1))
                reached_s = both[:, hd:]
                carried[g, j] = jnp.where(upper, both[:, :hd], held)
            else:
                reached_s = mm(carried[g, j], sib_s)
            states[bit, g, j] = jnp.where(upper, reached_s, 0.0).astype(BF)
            if more:
                sib = jnp.concatenate([sib_t, sib_s], axis=1).astype(F32)
                own = jnp.concatenate([send[bit, g, 0, j], send[bit, g, 1, j]], axis=1).astype(F32)
                first = jnp.where(upper, sib, own)
                second = jnp.where(upper, own, sib)
                merged = mm(second[:, :hd], first)
                send[bit + 1, g, 0, j] = merged[:, :hd].astype(BF)
                send[bit + 1, g, 1, j] = (merged[:, hd:] + second[:, hd:]).astype(BF)
        if more:
            copy(bit + 1, g).start()

    slots, late = exchange_slots(nbits, groups)

    def run_slot(at, part):
        for bit, g in slots.get((at, part), ()):
            exchange(bit, g)

    for at in range(groups):

        @pl.when(step == at)
        def _(at=at):
            copy(0, at).start()
            run_slot(at, 1)

    def read(which):
        read_half(
            which, step - groups, hs, doc_ref, q_ref, k_ref, v_ref, beta_ref, w_ref, inv_ref,
            erase_ref, y_ref, reader_ref, bias_ref, cum_ref,
        )

    for part in range(2):

        @pl.when((step >= groups) & (step < 2 * groups))
        def _(part=part):
            read(part)

        for at in range(groups, 2 * groups):
            if (at, part) in slots:

                @pl.when(step == at)
                def _(at=at, part=part):
                    run_slot(at, part)

    @pl.when(step == 2 * groups)
    def _():
        def finish(half_idx, g):
            finish_rows(half_idx, g, hs, low, y_ref, reader_ref, states, w_ref, gain_ref, z_ref)

        def finish_far(half_idx):
            for g in range(groups):
                for bit, owner in late:
                    if owner == g:
                        exchange(bit, owner)
                finish(half_idx, g)

        def finish_near(half_idx):
            lax.fori_loop(0, groups, lambda g, _: (finish(half_idx, g), 0)[1], 0)

        project_rows(
            me,
            finish_far,
            finish_near,
            weight_load,
            z_ref,
            weight_ref,
            out_ref,
            keep,
            (send_a, recv_a, send_y, recv_y, send_b, recv_b),
            (sa_sem, ra_sem, sy_sem, ry_sem, sb_sem, rb_sem),
        )
        for bit in range(nbits):
            for g in range(groups):
                copy(bit, g).wait_send()


def body(queries, keys, values, log_decay, beta, level_weights, doc_start, norm_gain, out_weight):
    tokens = queries.shape[0]
    heads = log_decay.shape[0]
    hd = queries.shape[1] // heads
    half = tokens // 2
    hs = 2
    groups = heads // hs
    low = (tokens // SPAN).bit_length()
    nbits = lax.axis_size("seq").bit_length() - 1
    wide = (tokens, hs * hd)
    rows = tokens // lax.axis_size("head")
    out_width = out_weight.shape[1]
    chunk = min(512, out_width)
    count = out_width // chunk

    def both(i):
        return (0, jnp.minimum(i, 2 * groups - 1) % groups)

    def second(i):
        return (0, jnp.clip(i - groups, 0, groups - 1))

    row_block = pl.BlockSpec((heads, tokens), lambda i: (0, 0))
    return pl.pallas_call(
        functools.partial(layer_kernel, hs, low),
        grid=(2 * groups + 1,),
        out_shape=jax.ShapeDtypeStruct((rows, out_width), BF),
        in_specs=[
            pl.BlockSpec(memory_space=pltpu.SMEM),
            pl.BlockSpec(wide, second),
            pl.BlockSpec(wide, both),
            pl.BlockSpec(wide, both),
            row_block,
            row_block,
            pl.BlockSpec(level_weights.shape, lambda i: (0, 0, 0)),
            pl.BlockSpec((1, heads * hd), lambda i: (0, 0)),
            pl.BlockSpec(memory_space=pl.ANY),
        ],
        out_specs=pl.BlockSpec((rows, out_width), lambda i: (0, 0)),
        scratch_shapes=[
            pltpu.VMEM((tokens, tokens), F32),
            pltpu.VMEM((heads, tokens), F32),
            pltpu.VMEM((groups, hs, 3, half, half), BF),
            pltpu.VMEM((groups, tokens, hs * hd), BF),
            pltpu.VMEM((groups, tokens, hs * hd), F32),
            pltpu.VMEM((groups, tokens, hs * hd), BF),
            pltpu.VMEM((nbits, groups, 2, hs, hd, hd), BF),
            pltpu.VMEM((nbits, groups, 2, hs, hd, hd), BF),
            pltpu.VMEM((groups, hs, hd, hd), F32),
            pltpu.VMEM((nbits, groups, hs, hd, hd), BF),
            pltpu.VMEM((tokens, heads * hd), BF),
            pltpu.VMEM(out_weight.shape, BF),
            pltpu.VMEM((2, count, rows, chunk), F32),
        ]
        + [pltpu.VMEM((count, rows, chunk), BF)] * 6
        + [pltpu.SemaphoreType.DMA((nbits, groups))] * 2
        + [pltpu.SemaphoreType.DMA((count,))] * 7,
        compiler_params=pltpu.CompilerParams(
            collective_id=0, has_side_effects=True, vmem_limit_bytes=56 * 2**20
        ),
        name="layer",
    )(
        doc_start, queries, keys, values, log_decay, beta, level_weights,
        norm_gain.reshape(1, -1), out_weight,
    )


def solution(mesh):
    placed = (
        P("seq", "head"),
        P("seq", "head"),
        P("seq", "head"),
        P("head", "seq"),
        P("head", "seq"),
        P(None, "head", "seq"),
        P("seq"),
        P("head"),
        P("head", None),
    )
    return jax.shard_map(
        body, mesh=mesh, in_specs=placed, out_specs=P(("seq", "head"), None), check_vma=False
    )
```

```python
import functools

import jax
import jax.numpy as jnp
from jax import lax
from jax.experimental import pallas as pl
from jax.experimental.pallas import tpu as pltpu
from jax.sharding import PartitionSpec as P

SPAN = 64
EPS = 1e-06
BF = jnp.bfloat16
F32 = jnp.float32


def mm(a, b):
    return jnp.dot(a.astype(BF), b.astype(BF), preferred_element_type=F32)


def mm_nt(a, b):
    return lax.dot_general(
        a.astype(BF), b.astype(BF), (((1,), (1,)), ((), ())), preferred_element_type=F32
    )


def mm_tn(a, b):
    return lax.dot_general(
        a.astype(BF), b.astype(BF), (((0,), (0,)), ((), ())), preferred_element_type=F32
    )


def normalize(vector):
    return vector * lax.rsqrt(jnp.sum(vector * vector, axis=-1, keepdims=True) + EPS)


def prefix_sum(rows):
    lane = lax.broadcasted_iota(jnp.int32, rows.shape, 1)
    reach = 1
    while reach < rows.shape[1]:
        rows = rows + jnp.where(lane >= reach, pltpu.roll(rows, reach, 1), 0.0)
        reach *= 2
    return rows


def document_ids(doc_ref, shape, dim):
    span = lax.broadcasted_iota(jnp.int32, shape, dim) // SPAN
    ids = jnp.zeros(shape, jnp.int32)
    for c in range(doc_ref.shape[0]):
        ids = ids + jnp.where(span >= c, doc_ref[c], 0)
    return ids


def fill_bias(doc_ref, bias_ref):
    tokens = bias_ref.shape[0]
    ids_col = document_ids(doc_ref, (tokens, 1), 0)
    ids_row = document_ids(doc_ref, (1, tokens), 1)
    rows = lax.broadcasted_iota(jnp.int32, (tokens, tokens), 0)
    cols = lax.broadcasted_iota(jnp.int32, (tokens, tokens), 1)
    valid = (rows >= cols) & (ids_col == ids_row)
    bias_ref[...] = jnp.where(valid, 0.0, -1e30)


def columns_of(rows):
    count, tokens = rows[0].shape[0] * len(rows), rows[0].shape[1]
    pad = -count % 8
    if pad:
        rows = rows + [jnp.zeros((pad, tokens), F32)]
    return jnp.concatenate(rows, axis=0).T


def pair_diagonal(pair):
    size = pair.shape[0]
    pair = pair.astype(BF)
    zero = jnp.zeros((size, size), BF)
    top = jnp.concatenate([pair[:, :size], zero], axis=1)
    return jnp.concatenate([top, jnp.concatenate([zero, pair[:, size:]], axis=1)], axis=0)


def unit_lower_inverses(pairs):
    size = pairs[0].shape[0]
    rows = lax.broadcasted_iota(jnp.int32, (size, 2 * size), 0)
    cols = lax.broadcasted_iota(jnp.int32, (size, 2 * size), 1)
    apart = rows ^ (cols % size)
    eye = jnp.where(apart == 0, 1.0, 0.0)
    base = 16
    inside = (apart < base) & (apart > 0)
    powers = [jnp.where(inside, pair, 0.0) for pair in pairs]
    inverses = [eye - power for power in powers]
    powers = [mm(power, pair_diagonal(power)) for power in powers]
    reach = 2
    while reach < base:
        if 2 * reach < base:
            both = [
                mm(
                    jnp.concatenate([power.astype(BF), inverse.astype(BF)], axis=0),
                    pair_diagonal(power),
                )
                for power, inverse in zip(powers, inverses)
            ]
            powers = [item[:size] for item in both]
            inverses = [inverse + item[size:] for inverse, item in zip(inverses, both)]
        else:
            inverses = [
                inverse + mm(inverse, pair_diagonal(power))
                for power, inverse in zip(powers, inverses)
            ]
        reach *= 2
    while base < size:
        band = (apart >= base) & (apart < 2 * base)
        offs = [pair_diagonal(jnp.where(band, pair, 0.0)) for pair in pairs]
        held = [inverse.astype(BF) for inverse in inverses]
        steps = [mm(inverse, off) for inverse, off in zip(held, offs)]
        steps = [mm(first, pair_diagonal(inverse)) for first, inverse in zip(steps, held)]
        inverses = [inverse - step for inverse, step in zip(inverses, steps)]
        base *= 2
    return [inverse.astype(BF) for inverse in inverses]


def form_maps(step, heads_step, doc_ref, k_ref, v_ref, beta_ref, inv_ref, erase_ref, map_ref, bias_ref, cum_ref):
    tokens = k_ref.shape[0]
    half = tokens // 2
    ids_col = document_ids(doc_ref, (tokens, 1), 0)
    first_doc = ids_col == 0
    last_doc = ids_col == jnp.max(ids_col)
    hd = 128
    eye = jnp.where(
        lax.broadcasted_iota(jnp.int32, (hd, hd), 0) == lax.broadcasted_iota(jnp.int32, (hd, hd), 1),
        1.0,
        0.0,
    )
    heads = range(heads_step)
    col_of = [slice(j * hd, (j + 1) * hd) for j in heads]
    keys = [normalize(k_ref[:, c].astype(F32)) for c in col_of]
    keys_b = [key.astype(BF) for key in keys]
    cum_rows = [cum_ref[pl.ds(step * heads_step + j, 1), :] for j in heads]
    sides = [
        columns_of([cum_rows[j], beta_ref[pl.ds(step * heads_step + j, 1), :]]) for j in heads
    ]
    cums, betas = [side[:, 0:1] for side in sides], [side[:, 1:2] for side in sides]
    quarter = half // 2
    parts = tokens // quarter

    def lower(j, rs, cs):
        ratio = jnp.exp(cums[j][rs] - cum_rows[j][:, cs] + bias_ref[rs, cs])
        return ratio * mm_nt(keys_b[j][rs], keys_b[j][cs]) * betas[j][rs]

    piece = [slice(i * quarter, (i + 1) * quarter) for i in range(parts)]
    merges = [(j, i) for j in heads for i in range(0, parts, 2)]
    paired = unit_lower_inverses(
        [
            jnp.concatenate([lower(j, piece[i + k], piece[i + k]) for k in range(2)], axis=1)
            for j, i in merges
        ]
    )
    diagonal = [pair[:, k * quarter : (k + 1) * quarter] for pair in paired for k in range(2)]
    firsts = [
        mm(diagonal[j * parts + i + 1], lower(j, piece[i + 1], piece[i])) for j, i in merges
    ]
    corners = [
        -mm(first, diagonal[j * parts + i]) for first, (j, i) in zip(firsts, merges)
    ]
    inverses = []
    for corner, (j, i) in zip(corners, merges):
        a, b = diagonal[j * parts + i], diagonal[j * parts + i + 1]
        top = jnp.concatenate([a, jnp.zeros_like(a)], axis=1)
        inverses.append(
            jnp.concatenate([top, jnp.concatenate([corner.astype(BF), b], axis=1)], axis=0)
        )
    low, high = slice(0, half), slice(half, tokens)
    firsts = [mm(inverses[2 * j + 1], lower(j, high, low)) for j in heads]
    cross = [(-mm(first, inverses[2 * j])).astype(BF) for j, first in enumerate(firsts)]
    for j in heads:
        c, key, cum, beta = col_of[j], keys[j], cums[j], betas[j]
        inv0, inv10, inv1 = inverses[2 * j], cross[j], inverses[2 * j + 1]
        inv_ref[step, j, 0] = inv0
        inv_ref[step, j, 1] = inv10
        inv_ref[step, j, 2] = inv1
        gamma = jnp.where(first_doc, jnp.exp(cum), 0.0)
        tail = jnp.where(last_doc, jnp.exp(cum_rows[j][:, tokens - 1 : tokens] - cum), 0.0)
        rhs = jnp.concatenate(
            [beta * v_ref[:, c].astype(F32), (beta * gamma) * key], axis=1
        ).astype(BF)
        solved0 = mm(inv0, rhs[:half])
        solved1 = mm(inv10, rhs[:half]) + mm(inv1, rhs[half:])
        solved = jnp.concatenate([solved0, solved1], axis=0).astype(BF)
        erase_ref[step, :, c] = solved[:, hd:]
        out = mm_tn(tail * key, solved)
        map_ref[0, step, 0, j] = (gamma[tokens - 1 : tokens, :] * eye - out[:, hd:]).astype(BF)
        map_ref[0, step, 1, j] = out[:, :hd].astype(BF)


def read_half(which, step, heads_step, doc_ref, q_ref, k_ref, v_ref, beta_ref, w_ref, inv_ref, erase_ref, y_ref, reader_ref, bias_ref, cum_ref):
    tokens = k_ref.shape[0]
    half = tokens // 2
    quarter = half // 2
    first = document_ids(doc_ref, (tokens, 1), 0) == 0
    hd = 128
    rows = lax.broadcasted_iota(jnp.int32, (quarter, quarter), 0)
    cols_i = lax.broadcasted_iota(jnp.int32, (quarter, quarter), 1)
    same_span = (rows ^ cols_i) < SPAN
    for j in range(heads_step):
        h = step * heads_step + j
        cols = slice(j * hd, (j + 1) * hd)
        key_b = normalize(k_ref[:, cols].astype(F32)).astype(BF)
        query = normalize(q_ref[:, cols].astype(F32))
        query_b = query.astype(BF)
        cum_row = cum_ref[pl.ds(h, 1), :]
        side = columns_of(
            [cum_row, beta_ref[pl.ds(h, 1), :]] + [w_ref[l, pl.ds(h, 1), :] for l in range(4)]
        )
        cum, beta = side[:, 0:1], side[:, 1:2]
        weights = [side[:, 2 + l : 3 + l] for l in range(4)]
        gamma = jnp.where(first, jnp.exp(cum), 0.0)

        def scores(r, c):
            rs, cs = slice(r * half, (r + 1) * half), slice(c * half, (c + 1) * half)
            ratio = jnp.exp(cum[rs] - cum_row[:, cs] + bias_ref[rs, cs])
            return (ratio * mm_nt(query_b[rs], key_b[cs])).astype(BF)

        def within(block, r):
            lo = r * half
            mid = lo + quarter
            a = block[:quarter, :quarter]
            a = a * jnp.where(same_span, weights[0][lo:mid], weights[1][lo:mid])
            b = block[quarter:, :quarter] * weights[2][mid : mid + quarter]
            c = block[quarter:, quarter:]
            c = c * jnp.where(
                same_span, weights[0][mid : mid + quarter], weights[1][mid : mid + quarter]
            )
            top = jnp.concatenate([a, jnp.zeros_like(a)], axis=1)
            return jnp.concatenate([top, jnp.concatenate([b, c], axis=1)], axis=0)

        inv0, inv10, inv1 = inv_ref[step, j, 0], inv_ref[step, j, 1], inv_ref[step, j, 2]
        value = (beta * v_ref[:, cols].astype(F32)).astype(BF)
        erase = erase_ref[step, :, cols]
        if which == 0:
            s00 = scores(0, 0)
            r00 = within(mm(s00, inv0), 0)
            y_ref[step, :half, cols] = mm(r00, value[:half])
            reader_ref[step, :half, cols] = (
                gamma[:half] * query[:half] - mm(s00, erase[:half])
            ).astype(BF)
            continue
        s10, s11 = scores(1, 0), scores(1, 1)
        r11 = within(mm(s11, inv1), 1)
        r10 = (mm(s10, inv0) + mm(s11, inv10)) * weights[3][half:]
        y_ref[step, half:, cols] = mm(r10, value[:half]) + mm(r11, value[half:])
        reader_ref[step, half:, cols] = (
            gamma[half:] * query[half:] - mm(s10, erase[:half]) - mm(s11, erase[half:])
        ).astype(BF)


def finish_rows(half_idx, g, hs, low, y_ref, reader_ref, state_ref, w_ref, gain_ref, z_ref):
    hd = 128
    levels = state_ref.shape[0]
    half = z_ref.shape[0] // 2
    part = pl.ds(pl.multiple_of(half_idx * half, half), half)

    for j in range(hs):
        h = g * hs + j
        cols = slice(j * hd, (j + 1) * hd)
        out_cols = pl.ds(pl.multiple_of(h * hd, hd), hd)
        side = columns_of([w_ref[low + l, pl.ds(h, 1), part] for l in range(levels)])
        y = y_ref[g, part, cols]
        reader = reader_ref[g, part, cols]
        for l in range(levels):
            y = y + side[:, l : l + 1] * mm(reader, state_ref[l, g, j])
        y = y * lax.rsqrt(jnp.mean(y * y, axis=-1, keepdims=True) + EPS)
        z_ref[part, out_cols] = (y * gain_ref[:, out_cols]).astype(BF)


def project_rows(is_far, me, weight_load, z_ref, w_ref, out_ref, keep, slabs, sems):
    mate = me + 1 - 2 * (me % 2)
    across = (me + 2) % 4
    send_a, recv_a, send_y, recv_y, send_b, recv_b = slabs
    sa_sem, ra_sem, sy_sem, ry_sem, sb_sem, rb_sem = sems
    count, rows, chunk = keep.shape[1:]
    near = me // 2
    far = 1 - near

    def columns(j):
        return pl.ds(pl.multiple_of(j * chunk, chunk), chunk)

    def remote(src, dst, ssem, rsem, j, target):
        return pltpu.make_async_remote_copy(
            src_ref=src.at[j],
            dst_ref=dst.at[j],
            send_sem=ssem.at[j],
            recv_sem=rsem.at[j],
            device_id={"head": target},
            device_id_type=pl.DeviceIdType.MESH,
        )

    def copy_a(j):
        return remote(send_a, recv_a, sa_sem, ra_sem, j, mate)

    def copy_b(j):
        return remote(send_b, recv_b, sb_sem, rb_sem, j, mate)

    def copy_y(j):
        return remote(send_y, recv_y, sy_sem, ry_sem, j, across)

    def terms(half_idx, j):
        part = pl.ds(pl.multiple_of(half_idx * 2 * rows, 2 * rows), 2 * rows)
        product = jnp.dot(z_ref[part, :], w_ref[:, columns(j)], preferred_element_type=F32)
        first = me % 2 == 0
        top, bottom = product[:rows], product[rows:]
        return jnp.where(first, top, bottom), jnp.where(first, bottom, top)

    def forward(j):
        copy_a(j).wait_recv()
        send_y[j] = (keep[0, j] + recv_a[j].astype(F32)).astype(BF)
        copy_y(j).start()

    def far_step(j, _):
        weight_load(j).wait()
        mine, other = terms(far, j)
        send_a[j] = other.astype(BF)
        copy_a(j).start()
        keep[0, j] = mine

        @pl.when(j > 0)
        def _():
            forward(j - 1)

        return 0

    def near_step(j, _):
        mine, other = terms(near, j)
        send_b[j] = other.astype(BF)
        copy_b(j).start()
        keep[1, j] = mine
        return 0

    def close(j, _):
        copy_b(j).wait_recv()
        copy_y(j).wait_recv()
        total = keep[1, j] + recv_b[j].astype(F32) + recv_y[j].astype(F32)
        out_ref[:, columns(j)] = total.astype(BF)
        copy_a(j).wait_send()
        copy_b(j).wait_send()
        copy_y(j).wait_send()
        return 0

    if is_far:
        lax.fori_loop(0, count, far_step, 0)
        forward(count - 1)
    else:
        lax.fori_loop(0, count, near_step, 0)
        lax.fori_loop(0, count, close, 0)


def exchange_slots(nbits, groups):
    form, read, hop = 4.4, 1.75, 3.4
    times = [(form * (at + 1), (at, 1)) for at in range(groups)]
    now = form * groups
    for at in range(groups, 2 * groups):
        now += read
        times.append((now, (at, 1)))
    slots, late = {}, []
    for g in range(groups):
        sent = form * (g + 1)
        for bit in range(nbits):
            open_slots = [(t, key) for t, key in times if sent is not None and t >= sent + hop]
            if open_slots:
                sent, key = open_slots[0]
                slots.setdefault(key, []).append((bit, g))
            else:
                sent = None
                late.append((bit, g))
    return slots, late


def layer_kernel(
    hs, low, doc_ref, q_ref, k_ref, v_ref, log_ref, beta_ref, w_ref, gain_ref, weight_hbm, out_ref,
    bias_ref, cum_ref, inv_ref, erase_ref, y_ref, reader_ref, send, recv, carried, states,
    z_ref, weight_ref, keep, send_a, recv_a, send_y, recv_y, send_b, recv_b,
    send_sem, recv_sem, load_sem, sa_sem, ra_sem, sy_sem, ry_sem, sb_sem, rb_sem,
):
    step = pl.program_id(0)
    nbits, groups = send.shape[0], send.shape[1]
    hd = send.shape[-1]
    block = lax.axis_index("seq")
    me = lax.axis_index("head")
    mate = me + 1 - 2 * (me % 2)
    across = (me + 2) % 4
    count, chunk = keep.shape[1], keep.shape[3]
    barrier = pltpu.get_barrier_semaphore()

    def partner(bit):
        return block + (1 << bit) * (1 - 2 * ((block // (1 << bit)) % 2))

    def copy(bit, g):
        whole = bit < nbits - 1
        return pltpu.make_async_remote_copy(
            src_ref=send.at[bit, g] if whole else send.at[bit, g, 1],
            dst_ref=recv.at[bit, g] if whole else recv.at[bit, g, 1],
            send_sem=send_sem.at[bit, g],
            recv_sem=recv_sem.at[bit, g],
            device_id={"seq": partner(bit)},
            device_id_type=pl.DeviceIdType.MESH,
        )

    def weight_load(j):
        cols = pl.ds(pl.multiple_of(j * chunk, chunk), chunk)
        return pltpu.make_async_copy(weight_hbm.at[:, cols], weight_ref.at[:, cols], load_sem.at[j])

    @pl.when(step == 0)
    def _():
        for other in (mate, across):
            pl.semaphore_signal(
                barrier, inc=1, device_id={"head": other}, device_id_type=pl.DeviceIdType.MESH
            )
        for bit in range(nbits):
            pl.semaphore_signal(
                barrier, inc=1, device_id={"seq": partner(bit)}, device_id_type=pl.DeviceIdType.MESH
            )
        fill_bias(doc_ref, bias_ref)
        cum_ref[...] = prefix_sum(log_ref[...])
        lax.fori_loop(0, count, lambda j, _: (weight_load(j).start(), 0)[1], 0)

    @pl.when(step < groups)
    def _():
        form_maps(
            step, hs, doc_ref, k_ref, v_ref, beta_ref, inv_ref, erase_ref, send, bias_ref, cum_ref
        )

    @pl.when(step == 0)
    def _():
        pl.semaphore_wait(barrier, nbits + 2)

    def exchange(bit, g):
        copy(bit, g).wait_recv()
        upper = (block // (1 << bit)) % 2 == 1
        eye = jnp.where(
            lax.broadcasted_iota(jnp.int32, (hd, hd), 0)
            == lax.broadcasted_iota(jnp.int32, (hd, hd), 1),
            1.0,
            0.0,
        )
        more = bit < nbits - 1
        for j in range(hs):
            sib_s = recv[bit, g, 1, j]
            if more:
                sib_t = recv[bit, g, 0, j]
            if bit == 0:
                reached_s = sib_s.astype(F32)
                if more:
                    carried[g, j] = jnp.where(upper, sib_t.astype(F32), eye)
            elif more:
                held = carried[g, j]
                both = mm(held, jnp.concatenate([sib_t, sib_s], axis=1))
                reached_s = both[:, hd:]
                carried[g, j] = jnp.where(upper, both[:, :hd], held)
            else:
                reached_s = mm(carried[g, j], sib_s)
            states[bit, g, j] = jnp.where(upper, reached_s, 0.0).astype(BF)
            if more:
                sib = jnp.concatenate([sib_t, sib_s], axis=1).astype(F32)
                own = jnp.concatenate([send[bit, g, 0, j], send[bit, g, 1, j]], axis=1).astype(F32)
                first = jnp.where(upper, sib, own)
                second = jnp.where(upper, own, sib)
                merged = mm(second[:, :hd], first)
                send[bit + 1, g, 0, j] = merged[:, :hd].astype(BF)
                send[bit + 1, g, 1, j] = (merged[:, hd:] + second[:, hd:]).astype(BF)
        if more:
            copy(bit + 1, g).start()

    slots, late = exchange_slots(nbits, groups)

    def run_slot(at, part):
        for bit, g in slots.get((at, part), ()):
            exchange(bit, g)

    for at in range(groups):

        @pl.when(step == at)
        def _(at=at):
            copy(0, at).start()
            run_slot(at, 1)

    far = 1 - me // 2
    near_start = 2 * groups + 1
    before = step < 2 * groups
    half_now = jnp.where(before, far, 1 - far)
    group_now = jnp.where(before, step - groups, step - near_start)
    reading = (step >= groups) & (step != 2 * groups) & (step < near_start + groups)

    for which in range(2):

        @pl.when(reading & (half_now == which))
        def _(which=which):
            read_half(
                which, group_now, hs, doc_ref, q_ref, k_ref, v_ref, beta_ref, w_ref, inv_ref,
                erase_ref, y_ref, reader_ref, bias_ref, cum_ref,
            )

    for at in range(groups, 2 * groups):
        if (at, 1) in slots:

            @pl.when(step == at)
            def _(at=at):
                run_slot(at, 1)

    def finish(half_idx, g):
        finish_rows(half_idx, g, hs, low, y_ref, reader_ref, states, w_ref, gain_ref, z_ref)

    def project(is_far):
        project_rows(
            is_far,
            me,
            weight_load,
            z_ref,
            weight_ref,
            out_ref,
            keep,
            (send_a, recv_a, send_y, recv_y, send_b, recv_b),
            (sa_sem, ra_sem, sy_sem, ry_sem, sb_sem, rb_sem),
        )

    @pl.when(step == 2 * groups)
    def _():
        for g in range(groups):
            for bit, owner in late:
                if owner == g:
                    exchange(bit, owner)
            finish(far, g)
        project(True)

    @pl.when((step >= near_start) & (step < near_start + groups))
    def _():
        finish(1 - far, group_now)

    @pl.when(step == near_start + groups)
    def _():
        project(False)
        for bit in range(nbits):
            for g in range(groups):
                copy(bit, g).wait_send()


def body(queries, keys, values, log_decay, beta, level_weights, doc_start, norm_gain, out_weight):
    tokens = queries.shape[0]
    heads = log_decay.shape[0]
    hd = queries.shape[1] // heads
    half = tokens // 2
    hs = 2
    groups = heads // hs
    low = (tokens // SPAN).bit_length()
    nbits = lax.axis_size("seq").bit_length() - 1
    wide = (tokens, hs * hd)
    rows = tokens // lax.axis_size("head")
    out_width = out_weight.shape[1]
    chunk = min(512, out_width)
    count = out_width // chunk

    def both(i):
        return (0, jnp.where(i < 2 * groups, i % groups, jnp.clip(i - 2 * groups - 1, 0, groups - 1)))

    def second(i):
        late = jnp.clip(i - 2 * groups - 1, 0, groups - 1)
        return (0, jnp.where(i < 2 * groups, jnp.clip(i - groups, 0, groups - 1), late))

    row_block = pl.BlockSpec((heads, tokens), lambda i: (0, 0))
    return pl.pallas_call(
        functools.partial(layer_kernel, hs, low),
        grid=(3 * groups + 2,),
        out_shape=jax.ShapeDtypeStruct((rows, out_width), BF),
        in_specs=[
            pl.BlockSpec(memory_space=pltpu.SMEM),
            pl.BlockSpec(wide, second),
            pl.BlockSpec(wide, both),
            pl.BlockSpec(wide, both),
            row_block,
            row_block,
            pl.BlockSpec(level_weights.shape, lambda i: (0, 0, 0)),
            pl.BlockSpec((1, heads * hd), lambda i: (0, 0)),
            pl.BlockSpec(memory_space=pl.ANY),
        ],
        out_specs=pl.BlockSpec((rows, out_width), lambda i: (0, 0)),
        scratch_shapes=[
            pltpu.VMEM((tokens, tokens), F32),
            pltpu.VMEM((heads, tokens), F32),
            pltpu.VMEM((groups, hs, 3, half, half), BF),
            pltpu.VMEM((groups, tokens, hs * hd), BF),
            pltpu.VMEM((groups, tokens, hs * hd), F32),
            pltpu.VMEM((groups, tokens, hs * hd), BF),
            pltpu.VMEM((nbits, groups, 2, hs, hd, hd), BF),
            pltpu.VMEM((nbits, groups, 2, hs, hd, hd), BF),
            pltpu.VMEM((groups, hs, hd, hd), F32),
            pltpu.VMEM((nbits, groups, hs, hd, hd), BF),
            pltpu.VMEM((tokens, heads * hd), BF),
            pltpu.VMEM(out_weight.shape, BF),
            pltpu.VMEM((2, count, rows, chunk), F32),
        ]
        + [pltpu.VMEM((count, rows, chunk), BF)] * 6
        + [pltpu.SemaphoreType.DMA((nbits, groups))] * 2
        + [pltpu.SemaphoreType.DMA((count,))] * 7,
        compiler_params=pltpu.CompilerParams(
            collective_id=0, has_side_effects=True, vmem_limit_bytes=56 * 2**20
        ),
        name="layer",
    )(
        doc_start, queries, keys, values, log_decay, beta, level_weights,
        norm_gain.reshape(1, -1), out_weight,
    )


def solution(mesh):
    placed = (
        P("seq", "head"),
        P("seq", "head"),
        P("seq", "head"),
        P("head", "seq"),
        P("head", "seq"),
        P(None, "head", "seq"),
        P("seq"),
        P("head"),
        P("head", None),
    )
    return jax.shard_map(
        body, mesh=mesh, in_specs=placed, out_specs=P(("seq", "head"), None), check_vma=False
    )
```
